256 devices in a mesh: src: 64 (over y, z, core), tgt: 4 (over x).
Axes of the slice: x: 4, y: 4, z: 8, core: 2. Of those that a mesh axis runs over, the one named last changes fastest.
Arguments:
- source_features: bfloat16 [524288, 64], P('src'), may hold values from -6 to 6
- target_features: bfloat16 [4, 8192, 64], P('tgt', 'src'), may hold values from -6 to 6
- block_targets: int32 [4096, 4, 8], P('src', 'tgt'), may hold values from -1 to 63, as said below
Outputs:
- source_dual: float32 [524288], P('src')
- target_dual: float32 [4, 8192], P('tgt', 'src')
The draws below stay inside these ranges and needn't reach their ends.
Inputs may be any that keep to these rules, and one draw needn't show every extreme that they name: `block_targets`: listed entries come first in each slot row and are distinct; every source block lists entry s mod 64 in every group, so every source cell and every target cell has allowed pairs; source block 0 lists 8 blocks in every group.
All inputs are finite; a program needn't handle non-finite values.
Results may differ from the reference program's by a relative error of at most 0.0009.
Values may be sent and summed in bfloat16 or wider, within the bound.
A program may use at most 64 MiB of HBM per device.

```python
import math
import jax
import jax.numpy as jnp
from jax import lax

BLK = 128
DIM = 64
TB_DEV = 64
KMAX = 8
ITERS = 2
SBLK = 4096
NS = 524288
TGT_SHARD = 8192
N_TGT = 4


def draw_block_targets(key, part):
    key = jax.random.fold_in(key, 7)
    order_key, count_key = jax.random.split(key)
    scores = jax.random.randint(order_key, (SBLK, N_TGT, TB_DEV - 1), 0, 1 << 20)
    order = jnp.argsort(scores, axis=-1, stable=True).astype(jnp.int32)
    source_block = jnp.arange(SBLK, dtype=jnp.int32)[:, None, None]
    others = (source_block + 1 + order[:, :, :KMAX - 1]) % TB_DEV
    first = jnp.broadcast_to(source_block % TB_DEV, (SBLK, N_TGT, 1))
    candidates = jnp.concatenate([first, others], axis=-1)
    counts = jax.random.randint(count_key, (SBLK, N_TGT, 1), 1, KMAX + 1)
    counts = jnp.where(source_block == 0, KMAX, counts)
    slot_number = jnp.arange(KMAX, dtype=jnp.int32)[None, None, :]
    return jnp.where(slot_number < counts, candidates, -1).astype(jnp.int32)


def level_of(stream_key, shape, cuts, low, top_value):
    gain, own = 1.0, jax.random.fold_in(stream_key, 6)
    for dim, shards_of in cuts:
        steps = jnp.exp(jax.random.uniform(jax.random.fold_in(own, dim), (shards_of,), jnp.float32, low / len(cuts), top_value / len(cuts)))
        gain = gain * jnp.repeat(steps, shape[dim] // shards_of).reshape([-1 if axis == dim else 1 for axis in range(len(shape))])
    return gain


def noise(key, dims, scale, bound, cuts=(), kind=jnp.bfloat16):
    result = jax.random.normal(key, dims, jnp.float32) * scale
    if len(cuts) > 0:
        result = level_of(key, dims, cuts, -0.22, 0.18) * result
    return jnp.clip(result, min=-bound, max=bound).astype(kind)


def setup_inputs(seed: int = 0) -> dict:
    splits = jax.random.split(jax.random.key(seed), 4)
    source_features = noise(splits[0], (NS, DIM), 1.0, 6.0, ((0, 64),))
    target_features = noise(splits[1], (N_TGT, TGT_SHARD, DIM), 1.0, 6.0, ((0, 4), (1, 64)))
    block_targets = draw_block_targets(jax.random.fold_in(splits[3], 71), 0)
    return dict(source_features=source_features, target_features=target_features, block_targets=block_targets)


EPSILON = 0.01
NEGATIVE = -1.0e30


def tile_costs(source_tile, target_tiles):
    source_f = source_tile.astype(jnp.float32)
    target_f = target_tiles.astype(jnp.float32)
    cross_term = jnp.einsum("gid,gkjd->gkij", source_f, target_f)
    source_sq = jnp.sum(source_f * source_f, axis=-1)
    target_sq = jnp.sum(target_f * target_f, axis=-1)
    return (source_sq[:, None, :, None] + target_sq[:, :, None, :] - 2.0 * cross_term) * (1.0 / source_tile.shape[-1])


def reference(source_features, target_features, block_targets):
    block_rows = block_targets.shape[0]
    shard_count = block_targets.shape[1]
    slot_count = block_targets.shape[2]
    target_blocks = target_features.shape[1] // BLK
    all_blocks = shard_count * target_blocks
    target_tiles = target_features.reshape(all_blocks, BLK, DIM)
    present = block_targets >= 0
    offsets = (jnp.arange(shard_count, dtype=jnp.int32) * target_blocks)[None, :, None]
    global_index = jnp.where(present, block_targets + offsets, 0).astype(jnp.int32)
    global_index = global_index.reshape(block_rows, shard_count * slot_count)
    present = present.reshape(block_rows, shard_count * slot_count)
    group_size = math.gcd(64, block_rows)
    turn_count = block_rows // group_size
    source_tiles = source_features.reshape(turn_count, group_size, BLK, DIM)
    index_groups = global_index.reshape(turn_count, group_size, -1)
    present_groups = present.reshape(turn_count, group_size, -1)
    log_source = -math.log(source_features.shape[0])
    log_target = -math.log(all_blocks * BLK)

    def row_half(target_dual):
        dual_tiles = target_dual.reshape(all_blocks, BLK)

        def one_group(operands):
            source_tile, index_tile, present_tile = operands
            costs = tile_costs(source_tile, target_tiles[index_tile])
            scores = (dual_tiles[index_tile][:, :, None, :] - costs) / EPSILON
            mask_tile = present_tile[:, :, None, None]
            scores = jnp.where(mask_tile, scores, NEGATIVE)
            peak = jnp.max(scores, axis=(1, 3))
            total = jnp.sum(jnp.where(mask_tile, jnp.exp(scores - peak[:, None, :, None]), 0.0), axis=(1, 3))
            return peak + jnp.log(total)

        lse_rows = lax.map(one_group, (source_tiles, index_groups, present_groups)).reshape(-1)
        return EPSILON * log_source - EPSILON * lse_rows

    def column_half(source_dual):
        dual_groups = source_dual.reshape(turn_count, group_size, BLK)

        def one_group(operands):
            source_tile, dual_tile, index_tile, present_tile = operands
            costs = tile_costs(source_tile, target_tiles[index_tile])
            scores = (dual_tile[:, None, :, None] - costs) / EPSILON
            mask_tile = present_tile[:, :, None, None]
            scores = jnp.where(mask_tile, scores, NEGATIVE)
            peak = jnp.max(scores, axis=2)
            total = jnp.sum(jnp.where(mask_tile, jnp.exp(scores - peak[:, :, None, :]), 0.0), axis=2)
            return peak, total

        peaks, totals = lax.map(one_group, (source_tiles, dual_groups, index_groups, present_groups))
        peaks = peaks.reshape(-1, BLK)
        totals = totals.reshape(-1, BLK)
        flat_index = jnp.where(present.reshape(-1), global_index.reshape(-1), all_blocks).astype(jnp.int32)
        safe_index = jnp.minimum(flat_index, all_blocks - 1)
        col_peak = jnp.full((all_blocks, BLK), NEGATIVE, jnp.float32).at[flat_index].max(peaks, mode="drop")
        shifted = totals * jnp.exp(peaks - col_peak[safe_index])
        col_total = jnp.zeros((all_blocks, BLK), jnp.float32).at[flat_index].add(shifted, mode="drop")
        dual = EPSILON * log_target - EPSILON * (col_peak + jnp.log(col_total))
        return dual.reshape(-1)

    target_dual = jnp.zeros((all_blocks * BLK,), jnp.float32)
    source_dual = jnp.zeros((source_features.shape[0],), jnp.float32)
    for iteration in range(ITERS):
        source_dual = row_half(target_dual)
        target_dual = column_half(source_dual)
    return source_dual, target_dual.reshape(shard_count, target_blocks * BLK)
```

```python
import functools
import math

import jax
import jax.numpy as jnp
from jax import lax
from jax.experimental import pallas as pl
from jax.experimental.pallas import tpu as pltpu
from jax.sharding import PartitionSpec as P

BLK = 128
DIM = 64
HALF = BLK // 2
NBLK = 64
SLOTS = 8
CHUNK = 4
STRIDE = NBLK + CHUNK
EPSILON = 0.01
NS = 524288
NT = 32768
NY, NZ, NX = 4, 8, 4
RATE = 2.0 / (DIM * EPSILON)
C2 = RATE / math.log(2.0)
LOG_NS = math.log(NS) / RATE
LOG_NT = math.log(NT) / RATE
LOW = -1.0e30
MAX_CHUNKS = 192
MESH = pl.DeviceIdType.MESH
VMEM = pl.BlockSpec(memory_space=pltpu.VMEM)
SMEM = pl.BlockSpec(memory_space=pltpu.SMEM)
f32, bf16 = jnp.float32, jnp.bfloat16


def iota(shape, dim):
    return lax.broadcasted_iota(jnp.int32, shape, dim)


def pieces(v):
    hi = v.astype(bf16).astype(f32)
    rest = v - hi
    mid = rest.astype(bf16).astype(f32)
    return hi, mid, rest - mid


def params(collective_id=None):
    if collective_id is None:
        return pltpu.CompilerParams(vmem_limit_bytes=40 << 20)
    return pltpu.CompilerParams(
        vmem_limit_bytes=40 << 20, collective_id=collective_id, has_side_effects=True
    )


def fold_potential(pot, aug):
    row = iota((HALF, BLK), 0)
    lane = iota((HALF, BLK), 1)
    pick = (lane % HALF == row).astype(bf16)
    n = iota((8, 16, BLK), 1)
    h = iota((8, 16, BLK), 2) // HALF
    keep = ((n < 6) & (n // 3 == h)) | ((n >= 6) & (n < 9) & (h == 0))
    for g in range(8):
        hi, mid, lo = (v[:, None, :] for v in pieces(pot[8 * g : 8 * g + 8, :]))
        rows = jnp.where(
            n >= 6, 1.0, jnp.where(n % 3 == 0, hi, jnp.where(n % 3 == 1, mid, lo))
        )
        rows = jnp.where(keep, rows, 0.0).reshape(BLK, BLK).astype(bf16)
        turned = lax.dot_general(pick, rows, (((1,), (1,)), ((), ())), preferred_element_type=f32)
        for k in range(8):
            aug[8 * g + k] = jnp.where(lane // 16 == k, turned, 0.0).astype(bf16)


def null_tile(aug):
    n = iota((HALF, BLK), 1)
    aug[NBLK] = jnp.where((n == 0) | (n == 3), LOW, 0.0).astype(bf16)


def weight_pattern():
    n = iota((16, BLK), 0)
    left = ((n < 3)).astype(bf16)
    right = ((n >= 3) & (n < 6)).astype(bf16)
    return left, right


def sweep(count, chunk_p, slots, lhs, aug, weights, pattern, pot_rows, bufs, process):
    left, right = pattern
    zero = jnp.zeros((DIM, BLK), bf16)

    def scores(n, buf):
        p = chunk_p[n]
        safe = jnp.minimum(p, NBLK - 1)
        ids = slots(n)
        w = weights(safe)
        if pot_rows is None:
            l16, r16 = left, right
        else:
            extra = pot_rows[safe]
            l16, r16 = left + extra, right + extra
        top = jnp.concatenate([w, zero], axis=1)
        mid = jnp.concatenate([zero, w], axis=1)
        low = jnp.concatenate([l16, r16], axis=1)
        rhs = jnp.concatenate([top, mid] + [low] * 8, axis=0)
        body = jnp.concatenate([lhs[jnp.minimum(q, NBLK - 1)] for q in ids], axis=0)
        tail = jnp.concatenate([aug[q] for q in ids], axis=0)
        both = jnp.concatenate([body, tail], axis=1)
        buf[...] = jnp.dot(both, rhs, preferred_element_type=f32)

    b0, b1, b2, b3 = bufs
    scores(0, b0)
    scores(1, b1)

    @pl.loop(0, (count + 3) // 4)
    def _(turn):
        n = 4 * turn
        scores(n + 2, b2)
        scores(n + 3, b3)
        process(n, chunk_p[n], b0)
        process(n + 1, chunk_p[n + 1], b1)
        scores(n + 4, b0)
        scores(n + 5, b1)
        process(n + 2, chunk_p[n + 2], b2)
        process(n + 3, chunk_p[n + 3], b3)


def max_process(peak, total):
    def process(n, p, buf):
        u = buf[...].reshape(CHUNK * HALF // 8, 8, 2 * BLK)
        top = jnp.max(u, axis=0)
        top = jnp.maximum(top[:, :BLK], top[:, BLK:])
        old = peak[p]
        new = jnp.maximum(old, top)
        new2 = jnp.concatenate([new, new], axis=1)
        e = jnp.sum(jnp.exp2((u - new2[None]) * C2), axis=0)
        peak[p] = new
        total[p] = total[p] * jnp.exp2((old - new) * C2) + (e[:, :BLK] + e[:, BLK:])

    return process


def sum_process(total):
    def process(n, p, buf):
        u = buf[...].reshape(CHUNK * HALF // 8, 8, 2 * BLK)
        e = jnp.sum(jnp.exp2(u * C2), axis=0)
        total[p] = total[p] + (e[:, :BLK] + e[:, BLK:])

    return process


def init_peaks(peak, total):
    peak[...] = jnp.full(peak.shape, LOW, f32)
    total[...] = jnp.zeros(total.shape, f32)


def finish_peaks(peak, total):
    m = peak[0:NBLK]
    top = jnp.max(m, axis=1)
    s = jnp.sum(total[0:NBLK] * jnp.exp2((m - top[:, None, :]) * C2), axis=1)
    return top + jnp.log2(s) * (1.0 / C2)


def row_chunks(bt, chunk_p, chunk_b):
    def step(p, n):
        chunk_p[n] = p
        chunk_b[n] = p * SLOTS
        more = (bt[p * SLOTS + CHUNK] >= 0).astype(jnp.int32)
        chunk_p[n + 1] = p
        chunk_b[n + 1] = p * SLOTS + CHUNK
        return n + 1 + more

    count = lax.fori_loop(0, NBLK, step, 0)
    for k in range(6):
        chunk_p[count + k] = NBLK
        chunk_b[count + k] = 0
    return count


def row_slots(bt, chunk_p, chunk_b):
    def slots(n):
        base, live = chunk_b[n], chunk_p[n] < NBLK
        ids = [bt[base + k] for k in range(CHUNK)]
        return [jnp.where((v >= 0) & live, v, NBLK) for v in ids]

    return slots


def col_chunks(lists, chunk_p, chunk_b):
    def step(t, n):
        size = lists[NBLK * STRIDE + t]
        for c in range(NBLK // CHUNK):
            chunk_p[n + c] = t
            chunk_b[n + c] = t * STRIDE + c * CHUNK
        return n + (size + CHUNK - 1) // CHUNK

    count = lax.fori_loop(0, NBLK, step, 0)
    for k in range(6):
        chunk_p[count + k] = NBLK
        chunk_b[count + k] = 0
    return count


def col_slots(lists, chunk_p, chunk_b):
    def slots(n):
        base, p = chunk_b[n], chunk_p[n]
        size = jnp.where(p < NBLK, lists[NBLK * STRIDE + jnp.minimum(p, NBLK - 1)], 0)
        first = base - p * STRIDE
        return [jnp.where(first + k < size, lists[base + k], NBLK) for k in range(CHUNK)]

    return slots


def row1_kernel(bt, yfold, xt, out, lists, aug, peak, total, chunk_p, chunk_b, b0, b1, b2, b3):
    k = iota((2 * BLK, BLK), 0) % BLK // DIM
    n = iota((2 * BLK, BLK), 1) % 16
    take = jnp.where((n < 6) & (n // 3 == k), -0.5, 0.0).astype(bf16)
    lane = iota((4 * HALF, BLK), 1)

    @pl.loop(0, NBLK // 4)
    def _(g):
        y = jnp.concatenate([yfold[4 * g + i] for i in range(4)], axis=0).astype(f32)
        sq = y * y
        hi = sq.astype(bf16)
        lo = (sq - hi.astype(f32)).astype(bf16)
        v = jnp.dot(jnp.concatenate([hi, lo], axis=1), take, preferred_element_type=f32)
        p0, p1, p2 = pieces(v)
        l = lane % 16
        v = jnp.where(l >= 6, jnp.where(l < 9, 1.0, 0.0), jnp.where(l % 3 == 0, p0, jnp.where(l % 3 == 1, p1, p2)))
        for i in range(4):
            part = v[i * HALF : (i + 1) * HALF]
            mine = lane[:HALF] // 16 == (4 * g + i) % 8
            aug[4 * g + i] = jnp.where(mine, part, 0.0).astype(bf16)

    null_tile(aug)
    init_peaks(peak, total)
    for t in range(NBLK + 1):
        lists[NBLK * STRIDE + t] = 0
    count = row_chunks(bt, chunk_p, chunk_b)
    slots = row_slots(bt, chunk_p, chunk_b)
    work = max_process(peak, total)

    def process(n, p, buf):
        for v in slots(n):
            at = lists[NBLK * STRIDE + v]
            at = jnp.where(v < NBLK, at, 0)
            lists[jnp.where(v < NBLK, v * STRIDE + at, NBLK * STRIDE + NBLK + 1)] = p
            lists[NBLK * STRIDE + v] = at + 1
        work(n, p, buf)

    sweep(
        count, chunk_p, slots, yfold, aug,
        lambda p: xt[:, pl.ds(pl.multiple_of(p * BLK, BLK), BLK)],
        weight_pattern(), None, (b0, b1, b2, b3), process,
    )
    out[...] = finish_peaks(peak, total)


def col1_kernel(lists, a, xfold, yt, out, aug, peak, total, chunk_p, chunk_b, b0, b1, b2, b3):
    fold_potential(a, aug)
    null_tile(aug)
    init_peaks(peak, total)
    count = col_chunks(lists, chunk_p, chunk_b)
    sweep(
        count, chunk_p, col_slots(lists, chunk_p, chunk_b), xfold, aug, lambda t: yt[t],
        weight_pattern(), None, (b0, b1, b2, b3), max_process(peak, total),
    )
    out[...] = finish_peaks(peak, total)


def spread_rows(pot, rows):
    n = iota((8, 16, BLK), 1)
    for g in range(8):
        hi, mid, lo = (v[:, None, :] for v in pieces(pot[8 * g : 8 * g + 8, :]))
        v = jnp.where(n == 6, hi, jnp.where(n == 7, mid, jnp.where(n == 8, lo, 0.0)))
        rows[8 * g : 8 * g + 8] = v.astype(bf16)


def row2_kernel(bt, a, b, yfold, xt, out, aug, rows, total, chunk_p, chunk_b, b0, b1, b2, b3):
    fold_potential(b, aug)
    null_tile(aug)
    spread_rows(a, rows)
    total[...] = jnp.zeros(total.shape, f32)
    count = row_chunks(bt, chunk_p, chunk_b)
    sweep(
        count, chunk_p, row_slots(bt, chunk_p, chunk_b), yfold, aug,
        lambda p: xt[:, pl.ds(pl.multiple_of(p * BLK, BLK), BLK)],
        weight_pattern(), rows, (b0, b1, b2, b3), sum_process(total),
    )
    out[...] = jnp.sum(total[0:NBLK], axis=1)


def col2_kernel(lists, a, b, xfold, yt, xt, out, f_out, aug, rows, total, chunk_p, chunk_b, b0, b1, b2, b3):
    fold_potential(a, aug)
    null_tile(aug)
    spread_rows(b, rows)
    total[...] = jnp.zeros(total.shape, f32)
    count = col_chunks(lists, chunk_p, chunk_b)

    @pl.loop(0, NBLK)
    def _(p):
        x = xt[:, pl.ds(pl.multiple_of(p * BLK, BLK), BLK)].astype(f32)
        sq = jnp.sum(x * x, axis=0, keepdims=True)
        f_out[pl.ds(p, 1), :] = a[pl.ds(p, 1), :] * (1.0 / 32) + sq * (1.0 / 64)

    sweep(
        count, chunk_p, col_slots(lists, chunk_p, chunk_b), xfold, aug, lambda t: yt[t],
        weight_pattern(), rows, (b0, b1, b2, b3), sum_process(total),
    )
    out[...] = jnp.sum(total[0:NBLK], axis=1)


def work_scratch(peaks, rows):
    acc = pltpu.VMEM((NBLK + 1, 8, BLK), f32)
    kinds = [pltpu.VMEM((NBLK + 1, HALF, BLK), bf16)]
    if rows:
        kinds.append(pltpu.VMEM((NBLK, 16, BLK), bf16))
    kinds += [acc] * (2 if peaks else 1)
    kinds += [pltpu.SMEM((MAX_CHUNKS + 16,), jnp.int32)] * 2
    kinds += [pltpu.VMEM((CHUNK * HALF, 2 * BLK), f32)] * 4
    return kinds


def duals(n=NBLK):
    return jax.ShapeDtypeStruct((n, BLK), f32)


def place():
    i = lax.axis_index("src")
    core, z, y = lax.rem(i, 2), lax.rem(i // 2, NZ), i // (2 * NZ)
    return y, z, core


def at(y, z, core):
    return {"src": (y * NZ + z) * 2 + core}


def greet(devices):
    barrier = pltpu.get_barrier_semaphore()
    for d in devices:
        pl.semaphore_signal(barrier, inc=1, device_id=d, device_id_type=MESH)
    pl.semaphore_wait(barrier, len(devices))


def send(src, dst, sends, recvs, k, device):
    copy = pltpu.make_async_remote_copy(
        src_ref=src, dst_ref=dst, send_sem=sends.at[k], recv_sem=recvs.at[k],
        device_id=device, device_id_type=MESH,
    )
    copy.start()
    return copy


def gather_kernel(y_ref, out, zs, zr, ys, yr, cs, cr, ls):
    y, z, core = place()
    z_devices = [at(y, lax.rem(z + k, NZ), core) for k in range(1, NZ)]
    y_devices = [at(lax.rem(y + k, NY), z, core) for k in range(1, NY)]
    mate = at(y, z, 1 - core)
    mine = pltpu.make_async_copy(y_ref, out.at[y, z, core], ls.at[0])
    mine.start()
    greet(z_devices + y_devices + [mate])
    copies = [send(y_ref, out.at[y, z, core], zs, zr, k, d) for k, d in enumerate(z_devices)]
    mine.wait()
    for c in copies:
        c.wait()
    copies = [
        send(out.at[y, :, core], out.at[y, :, core], ys, yr, k, d)
        for k, d in enumerate(y_devices)
    ]
    for c in copies:
        c.wait()
    last = send(out.at[:, :, core], out.at[:, :, core], cs, cr, 0, mate)
    last.wait()


def gather(tile):
    dma = pltpu.SemaphoreType.DMA
    return pl.pallas_call(
        gather_kernel,
        out_shape=jax.ShapeDtypeStruct((NY, NZ, 2, HALF, BLK), bf16),
        in_specs=[VMEM],
        out_specs=VMEM,
        scratch_shapes=[dma((7,)), dma((7,)), dma((3,)), dma((3,)), dma((1,)), dma((1,)), dma((1,))],
        compiler_params=params(0),
    )(tile)


def tgt_exchange(l_ref, got, sends, recvs):
    me = lax.axis_index("tgt")
    devices = [{"tgt": lax.rem(me + k, NX)} for k in range(1, NX)]
    greet(devices)
    copies = [send(l_ref, got.at[me], sends, recvs, k, d) for k, d in enumerate(devices)]
    got[me] = l_ref[...]
    for c in copies:
        c.wait()


def tgt1_kernel(l_ref, a_ref, got, sends, recvs):
    tgt_exchange(l_ref, got, sends, recvs)
    parts = [got[k] for k in range(NX)]
    top = functools.reduce(jnp.maximum, parts)
    s = sum(jnp.exp2((v - top) * C2) for v in parts)
    a_ref[...] = -(top + jnp.log2(s) * (1.0 / C2)) - LOG_NS


def tgt2_kernel(l_ref, old, a_ref, got, sends, recvs):
    tgt_exchange(l_ref, got, sends, recvs)
    s = (got[0] + got[1]) + (got[2] + got[3])
    a_ref[...] = old[...] - jnp.log2(s * NS) * (1.0 / C2)


def tgt_call(kernel, collective_id, *args):
    dma = pltpu.SemaphoreType.DMA
    return pl.pallas_call(
        kernel,
        out_shape=duals(),
        in_specs=[VMEM] * len(args),
        out_specs=VMEM,
        scratch_shapes=[pltpu.VMEM((NX, NBLK, BLK), f32), dma((3,)), dma((3,))],
        compiler_params=params(collective_id),
    )(*args)


def src_reduce(l_ref, combine, order, r1, rows, r2, s1, q1, s2, q2, more):
    y, z, core = place()
    m = y * 2 + core

    def side(k):
        other = lax.rem(m + k, 8)
        return other, at(other // 2, z, lax.rem(other, 2))

    def up(k):
        other = lax.rem(z + k, NZ)
        return other, at(y, other, core)

    sides, ups = [side(k) for k in range(1, 8)], [up(k) for k in range(1, 8)]
    for k in range(8):
        order[k] = l_ref[pl.ds((k // 2) * 2 * NZ + k % 2, NZ, stride=2), :]
    greet([d for _, d in sides + ups])
    copies = [send(order.at[o], r1.at[m], s1, q1, k, d) for k, (o, d) in enumerate(sides)]
    r1[m] = order[m]
    for c in copies:
        c.wait()
    first = combine([r1[k] for k in range(8)])
    for k in range(8):
        rows[k] = jnp.broadcast_to(first[k : k + 1], (8, BLK))
    copies = [send(rows.at[o], r2.at[z], s2, q2, k, d) for k, (o, d) in enumerate(ups)]
    r2[z] = rows[z]
    for c in copies:
        c.wait()
    return combine([r2[k] for k in range(8)]), m, z, sides, ups


def lse(parts):
    top = functools.reduce(jnp.maximum, parts)
    s = sum(jnp.exp2((v - top) * C2) for v in parts)
    return top + jnp.log2(s) * (1.0 / C2)


def src1_kernel(l_ref, b_ref, own_ref, order, r1, rows, r2, r3, tile, r4, s1, q1, s2, q2, s3, q3, s4, q4):
    total, m, z, sides, ups = src_reduce(l_ref, lse, order, r1, rows, r2, s1, q1, s2, q2, None)
    own_ref[...] = -total - LOG_NT
    copies = [send(own_ref, r3.at[z], s3, q3, k, d) for k, (_, d) in enumerate(ups)]
    r3[z] = own_ref[...]
    for c in copies:
        c.wait()
    tile[...] = jnp.concatenate([r3[k][0:1] for k in range(8)], axis=0)
    copies = [send(tile, r4.at[m], s4, q4, k, d) for k, (_, d) in enumerate(sides)]
    r4[m] = tile[...]
    for c in copies:
        c.wait()
    for k in range(8):
        b_ref[pl.ds((k // 2) * 2 * NZ + k % 2, NZ, stride=2), :] = r4[k]


def src2_kernel(l_ref, old, yt_ref, g_ref, order, r1, rows, r2, s1, q1, s2, q2):
    total = src_reduce(l_ref, sum, order, r1, rows, r2, s1, q1, s2, q2, None)[0]
    y = yt_ref[...].astype(f32)
    sq = jnp.sum(y * y, axis=0, keepdims=True)
    b = old[...] - jnp.log2(total * NT) * (1.0 / C2)
    g_ref[...] = b * (1.0 / 32) + sq * (1.0 / 64)


def src_scratch(phases):
    block = pltpu.VMEM((8, 8, BLK), f32)
    kinds = [block] * 4
    if phases == 4:
        kinds += [block, pltpu.VMEM((8, BLK), f32), block]
    return kinds + [pltpu.SemaphoreType.DMA((7,))] * (2 * phases)


def local(source_features, target_features, block_targets):
    xt = source_features.T
    yt_own = target_features[0].T
    bt = block_targets.reshape(-1)
    y_tile = target_features[0].reshape(2, HALF, DIM).transpose(1, 0, 2).reshape(HALF, BLK)
    xfold = source_features.reshape(NBLK, 2, HALF, DIM).transpose(0, 2, 1, 3).reshape(NBLK, HALF, BLK)
    yfold = gather(y_tile).reshape(NBLK, HALF, BLK)
    yt = yfold.reshape(NBLK, HALF, 2, DIM).transpose(0, 3, 2, 1).reshape(NBLK, DIM, BLK)

    row_lse, lists = pl.pallas_call(
        row1_kernel,
        out_shape=(duals(), jax.ShapeDtypeStruct((NBLK * STRIDE + 128,), jnp.int32)),
        in_specs=[SMEM, VMEM, VMEM],
        out_specs=(VMEM, SMEM),
        scratch_shapes=work_scratch(True, False),
        compiler_params=params(),
    )(bt, yfold, xt)
    a = tgt_call(tgt1_kernel, 1, row_lse)
    col_lse = pl.pallas_call(
        col1_kernel,
        out_shape=duals(),
        in_specs=[SMEM, VMEM, VMEM, VMEM],
        out_specs=VMEM,
        scratch_shapes=work_scratch(True, False),
        compiler_params=params(),
    )(lists, a, xfold, yt)
    b, own = pl.pallas_call(
        src1_kernel,
        out_shape=(duals(), duals(8)),
        in_specs=[VMEM],
        out_specs=(VMEM, VMEM),
        scratch_shapes=src_scratch(4),
        compiler_params=params(2),
    )(col_lse)
    row_sum = pl.pallas_call(
        row2_kernel,
        out_shape=duals(),
        in_specs=[SMEM, VMEM, VMEM, VMEM, VMEM],
        out_specs=VMEM,
        scratch_shapes=work_scratch(False, True),
        compiler_params=params(),
    )(bt, a, b, yfold, xt)
    a = tgt_call(tgt2_kernel, 3, row_sum, a)
    col_sum, f = pl.pallas_call(
        col2_kernel,
        out_shape=(duals(), duals()),
        in_specs=[SMEM, VMEM, VMEM, VMEM, VMEM, VMEM],
        out_specs=(VMEM, VMEM),
        scratch_shapes=work_scratch(False, True),
        compiler_params=params(),
    )(lists, a, b, xfold, yt, xt)
    g = pl.pallas_call(
        src2_kernel,
        out_shape=duals(8),
        in_specs=[VMEM, VMEM, VMEM],
        out_specs=VMEM,
        scratch_shapes=src_scratch(2),
        compiler_params=params(4),
    )(col_sum, own, yt_own)
    return f.reshape(-1), g[0:1]


def solution(mesh):
    in_specs = (P("src", None), P("tgt", "src", None), P("src", "tgt", None))
    out_specs = (P("src"), P("tgt", "src"))
    return jax.shard_map(local, mesh=mesh, in_specs=in_specs, out_specs=out_specs, check_vma=False)
```

```python
import functools
import math

import jax
import jax.numpy as jnp
from jax import lax
from jax.experimental import pallas as pl
from jax.experimental.pallas import tpu as pltpu
from jax.sharding import PartitionSpec as P

BLK = 128
DIM = 64
HALF = BLK // 2
NBLK = 64
SLOTS = 8
CHUNK = 4
STRIDE = NBLK + CHUNK
EPSILON = 0.01
NS = 524288
NT = 32768
NY, NZ, NX = 4, 8, 4
RATE = 2.0 / (DIM * EPSILON)
C2 = RATE / math.log(2.0)
LOG_NS = math.log(NS) / RATE
LOG_NT = math.log(NT) / RATE
LOW = -1.0e30
BODY = 16
MESH = pl.DeviceIdType.MESH
VMEM = pl.BlockSpec(memory_space=pltpu.VMEM)
SMEM = pl.BlockSpec(memory_space=pltpu.SMEM)
f32, bf16 = jnp.float32, jnp.bfloat16


def iota(shape, dim):
    return lax.broadcasted_iota(jnp.int32, shape, dim)


def pieces(v):
    hi = v.astype(bf16).astype(f32)
    rest = v - hi
    mid = rest.astype(bf16).astype(f32)
    return hi, mid, rest - mid


def params(collective_id=None):
    if collective_id is None:
        return pltpu.CompilerParams(vmem_limit_bytes=40 << 20)
    return pltpu.CompilerParams(
        vmem_limit_bytes=40 << 20, collective_id=collective_id, has_side_effects=True
    )


def picker():
    return (iota((HALF, BLK), 1) % HALF == iota((HALF, BLK), 0)).astype(bf16)


def turn_over(pick, rows):
    return lax.dot_general(pick, rows, (((1,), (1,)), ((), ())), preferred_element_type=f32)


def fold(pick, tile):
    low = (iota((DIM, BLK), 1) < HALF).astype(bf16)
    rows = jnp.concatenate([tile * low, tile * (1.0 - low).astype(bf16)], axis=0)
    return turn_over(pick, rows).astype(bf16)


def fold_potential(pot, aug):
    lane = iota((HALF, BLK), 1)
    pick = picker()
    n = iota((8, 16, BLK), 1)
    h = iota((8, 16, BLK), 2) // HALF
    keep = ((n < 6) & (n // 3 == h)) | ((n >= 6) & (n < 9) & (h == 0))
    for g in range(8):
        hi, mid, lo = (v[:, None, :] for v in pieces(pot[8 * g : 8 * g + 8, :]))
        rows = jnp.where(
            n >= 6, 1.0, jnp.where(n % 3 == 0, hi, jnp.where(n % 3 == 1, mid, lo))
        )
        rows = jnp.where(keep, rows, 0.0).reshape(BLK, BLK).astype(bf16)
        turned = turn_over(pick, rows)
        for k in range(8):
            aug[8 * g + k] = jnp.where(lane // 16 == k, turned, 0.0).astype(bf16)
    n = iota((HALF, BLK), 1)
    aug[NBLK] = jnp.where((n == 0) | (n == 3), LOW, 0.0).astype(bf16)


def spread_rows(pot, rows):
    n = iota((8, 16, BLK), 1)
    for g in range(8):
        hi, mid, lo = (v[:, None, :] for v in pieces(pot[8 * g : 8 * g + 8, :]))
        v = jnp.where(n == 6, hi, jnp.where(n == 7, mid, jnp.where(n == 8, lo, 0.0)))
        rows[8 * g : 8 * g + 8] = v.astype(bf16)


def sweep(chunks, slots, lhs, aug, weights, pot_rows, process):
    n16 = iota((16, BLK), 0)
    left = (n16 < 3).astype(bf16)
    right = ((n16 >= 3) & (n16 < 6)).astype(bf16)
    zero = jnp.zeros((DIM, BLK), bf16)

    @pl.loop(0, (chunks[0] + BODY - 1) // BODY)
    def _(turn):
        for k in range(BODY):
            n = BODY * turn + k
            p, base = chunks[1 + 2 * n], chunks[2 + 2 * n]
            safe = jnp.minimum(p, NBLK - 1)
            ids = slots(p, base)
            w = weights(safe)
            l16, r16 = left, right
            if pot_rows is not None:
                extra = pot_rows[safe]
                l16, r16 = left + extra, right + extra
            top = jnp.concatenate([w, zero], axis=1)
            mid = jnp.concatenate([zero, w], axis=1)
            low = jnp.concatenate([l16, r16], axis=1)
            rhs = jnp.concatenate([top, mid] + [low] * 8, axis=0)
            body = jnp.concatenate([lhs[jnp.minimum(q, NBLK - 1)] for q in ids], axis=0)
            tail = jnp.concatenate([aug[q] for q in ids], axis=0)
            both = jnp.concatenate([body, tail], axis=1)
            u = jnp.dot(both, rhs, preferred_element_type=f32)
            process(p, ids, u.reshape(CHUNK * HALF // 8, 8, 2 * BLK))


def max_process(peak, total):
    def process(p, ids, u):
        top = jnp.max(u, axis=0)
        top = jnp.maximum(top[:, :BLK], top[:, BLK:])
        old = peak[p]
        new = jnp.maximum(old, top)
        new2 = jnp.concatenate([new, new], axis=1)
        e = jnp.sum(jnp.exp2((u - new2[None]) * C2), axis=0)
        peak[p] = new
        total[p] = total[p] * jnp.exp2((old - new) * C2) + (e[:, :BLK] + e[:, BLK:])

    return process


def sum_process(total):
    def process(p, ids, u):
        e = jnp.sum(jnp.exp2(u * C2), axis=0)
        total[p] = total[p] + (e[:, :BLK] + e[:, BLK:])

    return process


def init_peaks(peak, total):
    peak[...] = jnp.full(peak.shape, LOW, f32)
    total[...] = jnp.zeros(total.shape, f32)


def finish_peaks(peak, total):
    m = peak[0:NBLK]
    top = jnp.max(m, axis=1)
    s = jnp.sum(total[0:NBLK] * jnp.exp2((m - top[:, None, :]) * C2), axis=1)
    return top + jnp.log2(s) * (1.0 / C2)


def finish_total(total):
    return jnp.sum(total[0:NBLK], axis=1)


def close_chunks(chunks, count):
    chunks[0] = count
    for k in range(BODY):
        chunks[1 + 2 * (count + k)] = NBLK
        chunks[2 + 2 * (count + k)] = 0


def row_chunks(bt, chunks):
    def step(p, n):
        for half in range(2):
            chunks[1 + 2 * (n + half)] = p
            chunks[2 + 2 * (n + half)] = p * SLOTS + half * CHUNK
        return n + 1 + (bt[p * SLOTS + CHUNK] >= 0).astype(jnp.int32)

    close_chunks(chunks, lax.fori_loop(0, NBLK, step, 0))


def row_slots(bt):
    def slots(p, base):
        ids = [bt[base + k] for k in range(CHUNK)]
        return [jnp.where((v >= 0) & (p < NBLK), v, NBLK) for v in ids]

    return slots


def col_chunks(lists, chunks):
    def step(t, n):
        many = (lists[NBLK * STRIDE + t] + CHUNK - 1) // CHUNK

        def put(c):
            chunks[1 + 2 * (n + c)] = t
            chunks[2 + 2 * (n + c)] = t * STRIDE + c * CHUNK

        put(0)
        put(1)

        @pl.when(many > 2)
        def _():
            pl.loop(2, many)(put)

        return n + many

    close_chunks(chunks, lax.fori_loop(0, NBLK, step, 0))


def col_slots(lists):
    def slots(p, base):
        size = jnp.where(p < NBLK, lists[NBLK * STRIDE + p], 0)
        first = base - p * STRIDE
        return [jnp.where(first + k < size, lists[base + k], NBLK) for k in range(CHUNK)]

    return slots


def x_weights(xt):
    return lambda p: xt[:, pl.ds(pl.multiple_of(p * BLK, BLK), BLK)]


def row1_kernel(bt, b, yfold, xt, peak, total, lists, chunks, cchunks, aug):
    fold_potential(b, aug)
    init_peaks(peak, total)
    for t in range(NBLK + 1):
        lists[NBLK * STRIDE + t] = 0
    row_chunks(bt, chunks)
    work = max_process(peak, total)

    def process(p, ids, u):
        for v in ids:
            real = v < NBLK
            have = jnp.where(real, lists[NBLK * STRIDE + v], 0)
            lists[jnp.where(real, v * STRIDE + have, NBLK * STRIDE + NBLK + 1)] = p
            lists[NBLK * STRIDE + v] = have + 1
        work(p, ids, u)

    sweep(chunks, row_slots(bt), yfold, aug, x_weights(xt), None, process)
    lists[NBLK * STRIDE + NBLK] = 0
    col_chunks(lists, cchunks)


def col1_kernel(lists, chunks, a, xfold, yt, peak, total, aug):
    fold_potential(a, aug)
    init_peaks(peak, total)
    sweep(chunks, col_slots(lists), xfold, aug, lambda t: yt[t], None, max_process(peak, total))


def row2_kernel(bt, chunks, a, b, yfold, xt, total, aug, rows):
    fold_potential(b, aug)
    spread_rows(a, rows)
    total[...] = jnp.zeros(total.shape, f32)
    sweep(chunks, row_slots(bt), yfold, aug, x_weights(xt), rows, sum_process(total))


def col2_kernel(lists, chunks, a, b, xfold, yt, xsq, total, f_out, aug, rows):
    fold_potential(a, aug)
    spread_rows(b, rows)
    total[...] = jnp.zeros(total.shape, f32)
    f_out[...] = a[...] * (1.0 / 32) + xsq[...] * (1.0 / 64)
    sweep(chunks, col_slots(lists), xfold, aug, lambda t: yt[t], rows, sum_process(total))


AUG = pltpu.VMEM((NBLK + 1, HALF, BLK), bf16)
ROWS = pltpu.VMEM((NBLK, 16, BLK), bf16)
ACC = jax.ShapeDtypeStruct((NBLK + 1, 8, BLK), f32)
LISTS = jax.ShapeDtypeStruct((NBLK * STRIDE + 128,), jnp.int32)
CHUNKS = jax.ShapeDtypeStruct((512,), jnp.int32)


def work_call(kernel, ins, outs, out_specs, scratch, *args):
    return pl.pallas_call(
        kernel,
        out_shape=outs,
        in_specs=ins,
        out_specs=out_specs,
        scratch_shapes=scratch,
        compiler_params=params(),
    )(*args)


def duals(n=NBLK):
    return jax.ShapeDtypeStruct((n, BLK), f32)


def place():
    i = lax.axis_index("src")
    core, z, y = lax.rem(i, 2), lax.rem(i // 2, NZ), i // (2 * NZ)
    return y, z, core


def at(y, z, core):
    return {"src": (y * NZ + z) * 2 + core}


def hail(devices):
    barrier = pltpu.get_barrier_semaphore()
    for d in devices:
        pl.semaphore_signal(barrier, inc=1, device_id=d, device_id_type=MESH)


def meet(devices):
    pl.semaphore_wait(pltpu.get_barrier_semaphore(), len(devices))


def send(src, dst, sends, recvs, k, device):
    copy = pltpu.make_async_remote_copy(
        src_ref=src, dst_ref=dst, send_sem=sends.at[k], recv_sem=recvs.at[k],
        device_id=device, device_id_type=MESH,
    )
    copy.start()
    return copy


def slot_of(dz):
    return 2 * dz - 1 if 0 < dz <= 4 else 2 * (NZ - dz) if dz else 0


GROUPS = ((0, 1), (1, 2), (3, 2), (5, 3))


def gather_kernel(own, xt, yt, yfold, b0, xfold, xsq, held, zs, zr, ys, yr, cs, cr):
    y, z, core = place()
    pick = picker()
    z_devices = {k: at(y, lax.rem(z + k, NZ), core) for k in range(1, NZ)}
    y_devices = {k: at(lax.rem(y + k, NY), z, core) for k in range(1, NY)}
    mate = at(y, z, 1 - core)
    everyone = list(z_devices.values()) + list(y_devices.values()) + [mate]
    hail(everyone)
    held[0, 0, 0] = own[...]
    meet(everyone)

    z_copies = {}
    for k in (4, 3, 5, 2, 6, 1, 7):
        z_copies[k] = send(own, held.at[0, 0, slot_of(NZ - k)], zs, zr, k - 1, z_devices[k])
    y_copies = {}

    def on_y(g):
        first, size = GROUPS[g]
        for k in (2, 1, 3):
            part = held.at[0, 0, pl.ds(first, size)]
            dst = held.at[0, NY - k, pl.ds(first, size)]
            y_copies[k, g] = send(part, dst, ys, yr, 4 * (k - 1) + g, y_devices[k])

    c_copies = []

    def on_mate(dy, first, size):
        part = held.at[0, dy, pl.ds(first, size)]
        dst = held.at[1, dy, pl.ds(first, size)]
        c_copies.append(send(part, dst, cs, cr, len(c_copies), mate))

    def fold_x(first, count):
        @pl.loop(first, first + count, step=4)
        def _(p):
            for i in range(4):
                tile = xt[:, pl.ds(pl.multiple_of((p + i) * BLK, BLK), BLK)]
                xfold[p + i] = fold(pick, tile)
                wide = tile.astype(f32)
                xsq[pl.ds(p + i, 1), :] = jnp.sum(wide * wide, axis=0, keepdims=True)

    def take(side, dy, first, count):
        @pl.loop(first, first + count)
        def _(s):
            back = lax.rem(s, 2)
            dz = back * ((s + 1) // 2) + (1 - back) * (NZ - s // 2)
            who = core if side == 0 else 1 - core
            t = (lax.rem(y + dy, NY) * NZ + lax.rem(z + dz, NZ)) * 2 + who
            tile = held[side, dy, s]
            yt[t] = tile
            yfold[t] = fold(pick, tile)
            wide = tile.astype(f32)
            b0[pl.ds(t, 1), :] = -0.5 * jnp.sum(wide * wide, axis=0, keepdims=True)

    on_y(0)
    fold_x(0, 32)
    for g, ks in ((1, (1, 7)), (2, (2, 6)), (3, (3, 5, 4))):
        for k in ks:
            z_copies[k].wait_recv()
        on_y(g)
        if g < 3:
            fold_x(16 + 16 * g, 16)
    on_mate(0, 0, NZ)
    take(0, 0, 0, NZ)
    for k in (1, 3, 2):
        for g in range(3):
            y_copies[k, g].wait_recv()
        on_mate(NY - k, 0, 5)
        take(0, NY - k, 0, 5)
    for k in (1, 3, 2):
        y_copies[k, 3].wait_recv()
        on_mate(NY - k, 5, 3)
        take(0, NY - k, 5, 3)
    c_copies[0].wait_recv()
    take(1, 0, 0, NZ)
    for i, k in enumerate((1, 3, 2)):
        c_copies[1 + i].wait_recv()
        take(1, NY - k, 0, 5)
    for i, k in enumerate((1, 3, 2)):
        c_copies[4 + i].wait_recv()
        take(1, NY - k, 5, 3)
    for c in list(z_copies.values()) + list(y_copies.values()) + c_copies:
        c.wait_send()


def gather(own, xt):
    dma = pltpu.SemaphoreType.DMA
    blocks = jax.ShapeDtypeStruct((NBLK, DIM, BLK), bf16)
    return pl.pallas_call(
        gather_kernel,
        out_shape=(blocks, blocks, duals(), blocks, duals()),
        in_specs=[VMEM] * 2,
        out_specs=(VMEM,) * 5,
        scratch_shapes=[pltpu.VMEM((2, NY, NZ, DIM, BLK), bf16)]
        + [dma((7,)), dma((7,)), dma((12,)), dma((12,)), dma((7,)), dma((7,))],
        compiler_params=params(0),
    )(own, xt)


def tgt_exchange(finish, mine, got, sends, recvs):
    me = lax.axis_index("tgt")
    devices = [{"tgt": lax.rem(me + k, NX)} for k in (2, 1, 3)]
    hail(devices)
    mine[...] = finish()
    meet(devices)
    copies = [send(mine, got.at[me], sends, recvs, k, d) for k, d in enumerate(devices)]
    got[me] = mine[...]
    for c in copies:
        c.wait()


def tgt1_kernel(peak, total, a_ref, mine, got, sends, recvs):
    tgt_exchange(lambda: finish_peaks(peak, total), mine, got, sends, recvs)
    a_ref[...] = -lse([got[k] for k in range(NX)]) - LOG_NS


def tgt2_kernel(total, old, a_ref, mine, got, sends, recvs):
    tgt_exchange(lambda: finish_total(total), mine, got, sends, recvs)
    s = (got[0] + got[1]) + (got[2] + got[3])
    a_ref[...] = old[...] - jnp.log2(s * NS) * (1.0 / C2)


def tgt_call(kernel, collective_id, *args):
    dma = pltpu.SemaphoreType.DMA
    mine = pltpu.VMEM((NBLK, BLK), f32)
    return pl.pallas_call(
        kernel,
        out_shape=duals(),
        in_specs=[VMEM] * len(args),
        out_specs=VMEM,
        scratch_shapes=[mine, pltpu.VMEM((NX, NBLK, BLK), f32), dma((3,)), dma((3,))],
        compiler_params=params(collective_id),
    )(*args)


def lse(parts):
    top = functools.reduce(jnp.maximum, parts)
    s = sum(jnp.exp2((v - top) * C2) for v in parts)
    return top + jnp.log2(s) * (1.0 / C2)


def mates():
    y, z, core = place()
    m = y * 2 + core

    def side(k):
        other = lax.rem(m + k, 8)
        return other, at(other // 2, z, lax.rem(other, 2))

    def up(k):
        other = lax.rem(z + k, NZ)
        return other, at(y, other, core)

    return m, z, [side(k) for k in range(1, 8)], [up(k) for k in (4, 3, 5, 2, 6, 1, 7)]


def rows_of(k):
    return pl.ds((k // 2) * 2 * NZ + k % 2, NZ, stride=2)


def scatter_sides(finish, combine, m, sides, ups, mine, order, r1, sends, recvs):
    devices = [d for _, d in ups + sides]
    hail(devices)
    mine[...] = finish()
    for k in range(8):
        order[k] = mine[rows_of(k), :]
    meet(devices)
    copies = [send(order.at[o], r1.at[m], sends, recvs, k, d) for k, (o, d) in enumerate(sides)]
    r1[m] = order[m]
    for c in copies:
        c.wait()
    return combine([r1[k] for k in range(8)])


def src1_kernel(peak, total, b_ref, own_ref, mine, order, r1, tile, r2, done, r4, s1, q1, s2, q2, s3, q3):
    m, z, sides, ups = mates()
    tile[...] = scatter_sides(
        lambda: finish_peaks(peak, total), lse, m, sides, ups, mine, order, r1, s1, q1
    )
    copies = [send(tile, r2.at[z], s2, q2, k, d) for k, (_, d) in enumerate(ups)]
    r2[z] = tile[...]
    for c in copies:
        c.wait()
    done[...] = -lse([r2[k] for k in range(8)]) - LOG_NT
    copies = [send(done, r4.at[m], s3, q3, k, d) for k, (_, d) in enumerate(sides)]
    r4[m] = done[...]
    own_ref[...] = jnp.broadcast_to(done[pl.ds(z, 1), :], (8, BLK))
    for c in copies:
        c.wait()
    for k in range(8):
        b_ref[rows_of(k), :] = r4[k]


def src2_kernel(total, old, yt_ref, g_ref, mine, order, r1, rows, r2, s1, q1, s2, q2):
    m, z, sides, ups = mates()
    first = scatter_sides(
        lambda: finish_total(total), sum, m, sides, ups, mine, order, r1, s1, q1
    )
    for k in range(8):
        rows[k] = jnp.broadcast_to(first[k : k + 1], (8, BLK))
    copies = [send(rows.at[o], r2.at[z], s2, q2, k, d) for k, (o, d) in enumerate(ups)]
    r2[z] = rows[z]
    y = yt_ref[...].astype(f32)
    sq = jnp.sum(y * y, axis=0, keepdims=True)
    for c in copies:
        c.wait()
    s = sum([r2[k] for k in range(8)])
    b = old[...] - jnp.log2(s * NT) * (1.0 / C2)
    g_ref[...] = b * (1.0 / 32) + sq * (1.0 / 64)


def src_call(kernel, collective_id, outs, scratch, phases, *args):
    mine = pltpu.VMEM((NBLK, BLK), f32)
    return pl.pallas_call(
        kernel,
        out_shape=outs,
        in_specs=[VMEM] * len(args),
        out_specs=jax.tree.map(lambda _: VMEM, outs),
        scratch_shapes=[mine] + scratch + [pltpu.SemaphoreType.DMA((7,))] * (2 * phases),
        compiler_params=params(collective_id),
    )(*args)


def local(source_features, target_features, block_targets):
    xt = source_features.T
    own_yt = target_features[0].T
    bt = block_targets.reshape(-1)
    block, tile = pltpu.VMEM((8, 8, BLK), f32), pltpu.VMEM((8, BLK), f32)

    yt, yfold, b0, xfold, xsq = gather(own_yt, xt)
    peak, total, lists, chunks, cchunks = work_call(
        row1_kernel, [SMEM, VMEM, VMEM, VMEM], (ACC, ACC, LISTS, CHUNKS, CHUNKS),
        (VMEM, VMEM, SMEM, SMEM, SMEM), [AUG], bt, b0, yfold, xt,
    )
    a = tgt_call(tgt1_kernel, 1, peak, total)
    peak, total = work_call(
        col1_kernel, [SMEM, SMEM, VMEM, VMEM, VMEM], (ACC, ACC), (VMEM, VMEM), [AUG],
        lists, cchunks, a, xfold, yt,
    )
    b, own = src_call(
        src1_kernel, 2, (duals(), duals(8)), [block, block, tile, block, tile, block], 3,
        peak, total,
    )
    total = work_call(
        row2_kernel, [SMEM, SMEM, VMEM, VMEM, VMEM, VMEM], ACC, VMEM, [AUG, ROWS],
        bt, chunks, a, b, yfold, xt,
    )
    a = tgt_call(tgt2_kernel, 3, total, a)
    total, f = work_call(
        col2_kernel, [SMEM, SMEM] + [VMEM] * 5, (ACC, duals()), (VMEM, VMEM), [AUG, ROWS],
        lists, cchunks, a, b, xfold, yt, xsq,
    )
    g = src_call(src2_kernel, 4, duals(8), [block] * 4, 2, total, own, own_yt)
    return f.reshape(-1), g[0:1]


def solution(mesh):
    in_specs = (P("src", None), P("tgt", "src", None), P("src", "tgt", None))
    out_specs = (P("src"), P("tgt", "src"))
    return jax.shard_map(local, mesh=mesh, in_specs=in_specs, out_specs=out_specs, check_vma=False)
```

```python
import functools
import math

import jax
import jax.numpy as jnp
from jax import lax
from jax.experimental import pallas as pl
from jax.experimental.pallas import tpu as pltpu
from jax.sharding import PartitionSpec as P

BLK = 128
DIM = 64
HALF = BLK // 2
NBLK = 64
SLOTS = 8
CHUNK = 2
LANES = 384
EPSILON = 0.01
NS = 524288
NT = 32768
NY, NZ, NX = 4, 8, 4
RATE = 2.0 / (DIM * EPSILON)
C2 = RATE / math.log(2.0)
LOG_NS = math.log(NS) / RATE
LOG_NT = math.log(NT) / RATE
LOW = -1.0e30
BODY = 48
MESH = pl.DeviceIdType.MESH
VMEM = pl.BlockSpec(memory_space=pltpu.VMEM)
SMEM = pl.BlockSpec(memory_space=pltpu.SMEM)
f32, bf16 = jnp.float32, jnp.bfloat16


def iota(shape, dim):
    return lax.broadcasted_iota(jnp.int32, shape, dim)


def pieces(v):
    hi = v.astype(bf16).astype(f32)
    rest = v - hi
    mid = rest.astype(bf16).astype(f32)
    return hi, mid, rest - mid


def params(collective_id=None):
    if collective_id is None:
        return pltpu.CompilerParams(vmem_limit_bytes=40 << 20)
    return pltpu.CompilerParams(
        vmem_limit_bytes=40 << 20, collective_id=collective_id, has_side_effects=True
    )


def picker():
    return (iota((HALF, BLK), 1) % HALF == iota((HALF, BLK), 0)).astype(bf16)


def turn_over(pick, rows):
    return lax.dot_general(pick, rows, (((1,), (1,)), ((), ())), preferred_element_type=f32)


def fold(pick, tile):
    low = (iota((DIM, BLK), 1) < HALF).astype(bf16)
    rows = jnp.concatenate([tile * low, tile * (1.0 - low).astype(bf16)], axis=0)
    return turn_over(pick, rows).astype(bf16)


def fold_potential(pot, aug):
    lane = iota((HALF, BLK), 1)
    pick = picker()
    n = iota((8, 16, BLK), 1)
    h = iota((8, 16, BLK), 2) // HALF
    keep = ((n < 6) & (n // 3 == h)) | ((n >= 6) & (n < 9) & (h == 0))
    for g in range(8):
        hi, mid, lo = (v[:, None, :] for v in pieces(pot[8 * g : 8 * g + 8, :]))
        rows = jnp.where(
            n >= 6, 1.0, jnp.where(n % 3 == 0, hi, jnp.where(n % 3 == 1, mid, lo))
        )
        rows = jnp.where(keep, rows, 0.0).reshape(BLK, BLK).astype(bf16)
        turned = turn_over(pick, rows)
        for k in range(8):
            aug[8 * g + k] = jnp.where(lane // 16 == k, turned, 0.0).astype(bf16)
    n = iota((HALF, BLK), 1)
    aug[NBLK] = jnp.where((n == 0) | (n == 3), LOW, 0.0).astype(bf16)


def spread_rows(pot, rows):
    n = iota((8, 16, BLK), 1)
    for g in range(8):
        hi, mid, lo = (v[:, None, :] for v in pieces(pot[8 * g : 8 * g + 8, :]))
        v = jnp.where(n == 6, hi, jnp.where(n == 7, mid, jnp.where(n == 8, lo, 0.0)))
        rows[8 * g : 8 * g + 8] = v.astype(bf16)


def chunk_table(member):
    dot = functools.partial(jnp.dot, preferred_element_type=f32)
    m = member.astype(bf16)
    up = (iota((NBLK, NBLK), 0) < iota((NBLK, NBLK), 1)).astype(bf16)
    upto = (iota((NBLK, NBLK), 0) >= iota((NBLK, NBLK), 1)).astype(bf16)
    eye = (iota((NBLK, NBLK), 0) == iota((NBLK, NBLK), 1)).astype(bf16)
    place_of = (member * (dot(m, up) + 1.0)).astype(bf16)
    turned = turn_over(eye, place_of).astype(bf16)
    size = dot(m, jnp.ones((NBLK, LANES), bf16))
    many = jnp.floor((size + (CHUNK - 1.0)) * (1.0 / CHUNK))
    end = dot(upto, many.astype(bf16))
    row = iota((NBLK, LANES), 0).astype(f32)
    n = iota((NBLK, LANES), 1).astype(f32)
    before = (end <= n).astype(f32)
    p = jnp.sum(before, axis=0, keepdims=True)
    first = CHUNK * (n[:1] - jnp.sum(before * many, axis=0, keepdims=True))
    mine = dot(turned, (row == p).astype(bf16))
    rows = [
        NBLK + jnp.sum((row - NBLK) * (mine == first + (k + 1.0)).astype(f32), axis=0, keepdims=True)
        for k in range(CHUNK)
    ]
    rows += [p, end[NBLK - 1 :]] + [jnp.zeros((1, LANES), f32)] * (6 - CHUNK)
    return jnp.concatenate(rows, axis=0).astype(jnp.int32)


def sweep(table, lhs, aug, weights, pot_rows, process):
    n16 = iota((16, BLK), 0)
    left = (n16 < 3).astype(bf16)
    right = ((n16 >= 3) & (n16 < 6)).astype(bf16)
    zero = jnp.zeros((DIM, BLK), bf16)

    @pl.loop(0, (table[3, 0] + BODY - 1) // BODY)
    def _(turn):
        for k in range(BODY):
            n = BODY * turn + k
            p = table[2, n]
            safe = jnp.minimum(p, NBLK - 1)
            ids = [table[i, n] for i in range(CHUNK)]
            w = weights(safe)
            l16, r16 = left, right
            if pot_rows is not None:
                extra = pot_rows[safe]
                l16, r16 = left + extra, right + extra
            top = jnp.concatenate([w, zero], axis=1)
            mid = jnp.concatenate([zero, w], axis=1)
            low = jnp.concatenate([l16, r16], axis=1)
            rhs = jnp.concatenate([top, mid] + [low] * 8, axis=0)
            body = jnp.concatenate([lhs[jnp.minimum(q, NBLK - 1)] for q in ids], axis=0)
            tail = jnp.concatenate([aug[q] for q in ids], axis=0)
            both = jnp.concatenate([body, tail], axis=1)
            process(p, jnp.dot(both, rhs, preferred_element_type=f32))


def max_process(peak, total):
    def process(p, v):
        old, sums = peak[p], total[p]
        for k in range(CHUNK):
            u = v[k * HALF : (k + 1) * HALF].reshape(HALF // 8, 8, 2 * BLK)
            top = jnp.max(u, axis=0)
            new = jnp.maximum(old, jnp.maximum(top[:, :BLK], top[:, BLK:]))
            new2 = jnp.concatenate([new, new], axis=1)
            e = jnp.sum(jnp.exp2((u - new2[None]) * C2), axis=0)
            sums = sums * jnp.exp2((old - new) * C2) + (e[:, :BLK] + e[:, BLK:])
            old = new
        peak[p] = old
        total[p] = sums

    return process


def sum_process(total):
    def process(p, v):
        u = v.reshape(CHUNK * HALF // 8, 8, 2 * BLK)
        e = jnp.sum(jnp.exp2(u * C2), axis=0)
        total[p] = total[p] + (e[:, :BLK] + e[:, BLK:])

    return process


def init_peaks(peak, total):
    peak[...] = jnp.full(peak.shape, LOW, f32)
    total[...] = jnp.zeros(total.shape, f32)


def finish_peaks(peak, total):
    m = peak[0:NBLK]
    top = jnp.max(m, axis=1)
    s = jnp.sum(total[0:NBLK] * jnp.exp2((m - top[:, None, :]) * C2), axis=1)
    return top + jnp.log2(s) * (1.0 / C2)


def finish_total(total):
    return jnp.sum(total[0:NBLK], axis=1)


def x_weights(xt):
    return lambda p: xt[:, pl.ds(pl.multiple_of(p * BLK, BLK), BLK)]


def row1_kernel(table, b, yfold, xt, peak, total, aug):
    fold_potential(b, aug)
    init_peaks(peak, total)
    sweep(table, yfold, aug, x_weights(xt), None, max_process(peak, total))


def col1_kernel(table, a, xfold, yt, peak, total, aug):
    fold_potential(a, aug)
    init_peaks(peak, total)
    sweep(table, xfold, aug, lambda t: yt[t], None, max_process(peak, total))


def row2_kernel(table, rows, b, yfold, xt, total, aug):
    fold_potential(b, aug)
    total[...] = jnp.zeros(total.shape, f32)
    sweep(table, yfold, aug, x_weights(xt), rows, sum_process(total))


def col2_kernel(table, rows, a, xfold, yt, xsq, total, f_out, aug):
    fold_potential(a, aug)
    total[...] = jnp.zeros(total.shape, f32)
    f_out[...] = a[...] * (1.0 / 32) + xsq[...] * (1.0 / 64)
    sweep(table, xfold, aug, lambda t: yt[t], rows, sum_process(total))


AUG = pltpu.VMEM((NBLK + 1, HALF, BLK), bf16)
ROWS = jax.ShapeDtypeStruct((NBLK, 16, BLK), bf16)
ACC = jax.ShapeDtypeStruct((NBLK + 1, 8, BLK), f32)
TABLE = jax.ShapeDtypeStruct((8, LANES), jnp.int32)


def work_call(kernel, outs, *args):
    return pl.pallas_call(
        kernel,
        out_shape=outs,
        in_specs=[SMEM] + [VMEM] * (len(args) - 1),
        out_specs=jax.tree.map(lambda _: VMEM, outs),
        scratch_shapes=[AUG],
        compiler_params=params(),
    )(*args)


def duals(n=NBLK):
    return jax.ShapeDtypeStruct((n, BLK), f32)


def place():
    i = lax.axis_index("src")
    core, z, y = lax.rem(i, 2), lax.rem(i // 2, NZ), i // (2 * NZ)
    return y, z, core


def at(y, z, core):
    return {"src": (y * NZ + z) * 2 + core}


def hail(devices):
    barrier = pltpu.get_barrier_semaphore()
    for d in devices:
        pl.semaphore_signal(barrier, inc=1, device_id=d, device_id_type=MESH)


def meet(devices):
    pl.semaphore_wait(pltpu.get_barrier_semaphore(), len(devices))


def send(src, dst, sends, recvs, k, device):
    copy = pltpu.make_async_remote_copy(
        src_ref=src, dst_ref=dst, send_sem=sends.at[k], recv_sem=recvs.at[k],
        device_id=device, device_id_type=MESH,
    )
    copy.start()
    return copy


def slot_of(dz):
    return 2 * dz - 1 if 0 < dz <= 4 else 2 * (NZ - dz) if dz else 0


GROUPS = ((0, 1), (1, 2), (3, 2), (5, 3))


def gather_kernel(own, bt, yt, yfold, b0, row_table, col_table, held, zs, zr, ys, yr, cs, cr):
    y, z, core = place()
    pick = picker()
    z_devices = {k: at(y, lax.rem(z + k, NZ), core) for k in (4, 3, 5, 2, 6, 1, 7)}
    y_devices = {k: at(lax.rem(y + k, NY), z, core) for k in (2, 1, 3)}
    mate = at(y, z, 1 - core)
    everyone = list(z_devices.values()) + list(y_devices.values()) + [mate]
    hail(everyone)
    held[0, 0, 0] = own[...]
    meet(everyone)

    z_copies = {}
    for k, d in z_devices.items():
        z_copies[k] = send(own, held.at[0, 0, slot_of(NZ - k)], zs, zr, k - 1, d)
    y_copies = {}

    def on_y(g):
        first, size = GROUPS[g]
        for k, d in y_devices.items():
            part = held.at[0, 0, pl.ds(first, size)]
            dst = held.at[0, NY - k, pl.ds(first, size)]
            y_copies[k, g] = send(part, dst, ys, yr, 4 * (k - 1) + g, d)

    c_copies = []

    def on_mate(dy, dys, first, size):
        part = held.at[0, pl.ds(dy, dys), pl.ds(first, size)]
        dst = held.at[1, pl.ds(dy, dys), pl.ds(first, size)]
        c_copies.append(send(part, dst, cs, cr, len(c_copies), mate))

    def take(side, dy, s):
        back = lax.rem(s, 2)
        dz = back * ((s + 1) // 2) + (1 - back) * (NZ - s // 2)
        who = core if side == 0 else 1 - core
        t = (lax.rem(y + dy, NY) * NZ + lax.rem(z + dz, NZ)) * 2 + who
        tile = held[side, dy, s]
        yt[t] = tile
        yfold[t] = fold(pick, tile)
        wide = tile.astype(f32)
        b0[pl.ds(t, 1), :] = -0.5 * jnp.sum(wide * wide, axis=0, keepdims=True)

    def take_column(side):
        @pl.loop(0, NZ, step=4)
        def _(s):
            for i in range(4):
                take(side, 0, s + i)

    def take_group(side, g):
        @pl.loop(GROUPS[g][0], GROUPS[g][0] + GROUPS[g][1])
        def _(s):
            for dy in range(1, NY):
                take(side, dy, s)

    on_y(0)
    t = iota((NBLK, NBLK), 0)
    member = sum((bt[k : k + 1, :] == t).astype(f32) for k in range(SLOTS))
    col_table[...] = chunk_table(member)
    eye = (iota((NBLK, NBLK), 1) == t).astype(bf16)
    row_table[...] = chunk_table(turn_over(eye, member.astype(bf16)))
    for g, ks in ((1, (1, 7)), (2, (2, 6)), (3, (3, 5, 4))):
        for k in ks:
            z_copies[k].wait_recv()
        on_y(g)
    on_mate(0, 1, 0, NZ)
    for g in range(4):
        for k in (1, 3, 2):
            y_copies[k, g].wait_recv()
        on_mate(1, NY - 1, *GROUPS[g])
        if g == 0:
            take_column(0)
        take_group(0, g)
    c_copies[0].wait_recv()
    take_column(1)
    for g in range(4):
        c_copies[1 + g].wait_recv()
        take_group(1, g)
    for c in list(z_copies.values()) + list(y_copies.values()) + c_copies:
        c.wait_send()


def gather(own, bt):
    dma = pltpu.SemaphoreType.DMA
    blocks = jax.ShapeDtypeStruct((NBLK, DIM, BLK), bf16)
    return pl.pallas_call(
        gather_kernel,
        out_shape=(blocks, blocks, duals(), TABLE, TABLE),
        in_specs=[VMEM] * 2,
        out_specs=(VMEM,) * 5,
        scratch_shapes=[pltpu.VMEM((2, NY, NZ, DIM, BLK), bf16)]
        + [dma((7,)), dma((7,)), dma((12,)), dma((12,)), dma((5,)), dma((5,))],
        compiler_params=params(0),
    )(own, bt)


def tgt_exchange(finish, meanwhile, mine, got, sends, recvs):
    me = lax.axis_index("tgt")
    devices = [{"tgt": lax.rem(me + k, NX)} for k in (2, 1, 3)]
    hail(devices)
    mine[...] = finish()
    meet(devices)
    copies = [send(mine, got.at[me], sends, recvs, k, d) for k, d in enumerate(devices)]
    got[me] = mine[...]
    meanwhile()
    for c in copies:
        c.wait()


def tgt1_kernel(peak, total, xt, a_ref, xfold, xsq, mine, got, sends, recvs):
    pick = picker()

    def fold_x():
        @pl.loop(0, NBLK, step=8)
        def _(p):
            for i in range(8):
                tile = xt[:, pl.ds(pl.multiple_of((p + i) * BLK, BLK), BLK)]
                xfold[p + i] = fold(pick, tile)
                wide = tile.astype(f32)
                xsq[pl.ds(p + i, 1), :] = jnp.sum(wide * wide, axis=0, keepdims=True)

    tgt_exchange(lambda: finish_peaks(peak, total), fold_x, mine, got, sends, recvs)
    a_ref[...] = -lse([got[k] for k in range(NX)]) - LOG_NS


def tgt2_kernel(total, old, b_ref, a_ref, rows, mine, got, sends, recvs):
    tgt_exchange(
        lambda: finish_total(total), lambda: spread_rows(b_ref, rows), mine, got, sends, recvs
    )
    s = (got[0] + got[1]) + (got[2] + got[3])
    a_ref[...] = old[...] - jnp.log2(s * NS) * (1.0 / C2)


def tgt_call(kernel, collective_id, outs, *args):
    dma = pltpu.SemaphoreType.DMA
    mine = pltpu.VMEM((NBLK, BLK), f32)
    return pl.pallas_call(
        kernel,
        out_shape=outs,
        in_specs=[VMEM] * len(args),
        out_specs=jax.tree.map(lambda _: VMEM, outs),
        scratch_shapes=[mine, pltpu.VMEM((NX, NBLK, BLK), f32), dma((3,)), dma((3,))],
        compiler_params=params(collective_id),
    )(*args)


def lse(parts):
    top = functools.reduce(jnp.maximum, parts)
    s = sum(jnp.exp2((v - top) * C2) for v in parts)
    return top + jnp.log2(s) * (1.0 / C2)


def mates():
    y, z, core = place()
    m = y * 2 + core

    def side(k):
        other = lax.rem(m + k, 8)
        return other, at(other // 2, z, lax.rem(other, 2))

    def up(k):
        other = lax.rem(z + k, NZ)
        return other, at(y, other, core)

    return m, z, [side(k) for k in range(1, 8)], [up(k) for k in (4, 3, 5, 2, 6, 1, 7)]


def rows_of(k):
    return pl.ds((k // 2) * 2 * NZ + k % 2, NZ, stride=2)


def scatter_sides(finish, combine, m, sides, ups, mine, order, r1, sends, recvs):
    devices = [d for _, d in ups + sides]
    hail(devices)
    mine[...] = finish()
    for k in range(8):
        order[k] = mine[rows_of(k), :]
    meet(devices)
    copies = [send(order.at[o], r1.at[m], sends, recvs, k, d) for k, (o, d) in enumerate(sides)]
    r1[m] = order[m]
    for c in copies:
        c.wait()
    return combine([r1[k] for k in range(8)])


def src1_kernel(peak, total, a_ref, b_ref, own_ref, spread, mine, order, r1, tile, r2, done, r4, s1, q1, s2, q2, s3, q3):
    m, z, sides, ups = mates()
    tile[...] = scatter_sides(
        lambda: finish_peaks(peak, total), lse, m, sides, ups, mine, order, r1, s1, q1
    )
    copies = [send(tile, r2.at[z], s2, q2, k, d) for k, (_, d) in enumerate(ups)]
    r2[z] = tile[...]
    spread_rows(a_ref, spread)
    for c in copies:
        c.wait()
    done[...] = -lse([r2[k] for k in range(8)]) - LOG_NT
    copies = [send(done, r4.at[m], s3, q3, k, d) for k, (_, d) in enumerate(sides)]
    r4[m] = done[...]
    own_ref[...] = jnp.broadcast_to(done[pl.ds(z, 1), :], (8, BLK))
    for c in copies:
        c.wait()
    for k in range(8):
        b_ref[rows_of(k), :] = r4[k]


def src2_kernel(total, old, yt_ref, g_ref, mine, order, r1, rows, r2, s1, q1, s2, q2):
    m, z, sides, ups = mates()
    first = scatter_sides(
        lambda: finish_total(total), sum, m, sides, ups, mine, order, r1, s1, q1
    )
    for k in range(8):
        rows[k] = jnp.broadcast_to(first[k : k + 1], (8, BLK))
    copies = [send(rows.at[o], r2.at[z], s2, q2, k, d) for k, (o, d) in enumerate(ups)]
    r2[z] = rows[z]
    y = yt_ref[...].astype(f32)
    sq = jnp.sum(y * y, axis=0, keepdims=True)
    for c in copies:
        c.wait()
    s = sum([r2[k] for k in range(8)])
    b = old[...] - jnp.log2(s * NT) * (1.0 / C2)
    g_ref[...] = b * (1.0 / 32) + sq * (1.0 / 64)


def src_call(kernel, collective_id, outs, scratch, phases, *args):
    mine = pltpu.VMEM((NBLK, BLK), f32)
    return pl.pallas_call(
        kernel,
        out_shape=outs,
        in_specs=[VMEM] * len(args),
        out_specs=jax.tree.map(lambda _: VMEM, outs),
        scratch_shapes=[mine] + scratch + [pltpu.SemaphoreType.DMA((7,))] * (2 * phases),
        compiler_params=params(collective_id),
    )(*args)


def local(source_features, target_features, block_targets):
    own_yt = target_features[0].T
    block, tile = pltpu.VMEM((8, 8, BLK), f32), pltpu.VMEM((8, BLK), f32)

    xt = source_features.T
    blocks = jax.ShapeDtypeStruct((NBLK, DIM, BLK), bf16)
    yt, yfold, b0, row_table, col_table = gather(own_yt, block_targets[:, 0, :].T)
    peak, total = work_call(row1_kernel, (ACC, ACC), row_table, b0, yfold, xt)
    a, xfold, xsq = tgt_call(tgt1_kernel, 1, (duals(), blocks, duals()), peak, total, xt)
    peak, total = work_call(col1_kernel, (ACC, ACC), col_table, a, xfold, yt)
    b, own, rows = src_call(
        src1_kernel, 2, (duals(), duals(8), ROWS), [block, block, tile, block, tile, block], 3,
        peak, total, a,
    )
    total = work_call(row2_kernel, ACC, row_table, rows, b, yfold, xt)
    a, rows = tgt_call(tgt2_kernel, 3, (duals(), ROWS), total, a, b)
    total, f = work_call(col2_kernel, (ACC, duals()), col_table, rows, a, xfold, yt, xsq)
    g = src_call(src2_kernel, 4, duals(8), [block] * 4, 2, total, own, own_yt)
    return f.reshape(-1), g[0:1]


def solution(mesh):
    in_specs = (P("src", None), P("tgt", "src", None), P("src", "tgt", None))
    out_specs = (P("src"), P("tgt", "src"))
    return jax.shard_map(local, mesh=mesh, in_specs=in_specs, out_specs=out_specs, check_vma=False)
```

```python
import functools
import math

import jax
import jax.numpy as jnp
from jax import lax
from jax.experimental import pallas as pl
from jax.experimental.pallas import tpu as pltpu
from jax.sharding import PartitionSpec as P

BLK = 128
DIM = 64
HALF = BLK // 2
NBLK = 64
SLOTS = 8
CHUNK = 2
LANES = 384
EPSILON = 0.01
NS = 524288
NT = 32768
NY, NZ, NX = 4, 8, 4
RATE = 2.0 / (DIM * EPSILON)
C2 = RATE / math.log(2.0)
LOG_NS = math.log(NS) / RATE
LOG_NT = math.log(NT) / RATE
LOW = -1.0e30
BODY = 96
MESH = pl.DeviceIdType.MESH
VMEM = pl.BlockSpec(memory_space=pltpu.VMEM)
SMEM = pl.BlockSpec(memory_space=pltpu.SMEM)
f32, bf16 = jnp.float32, jnp.bfloat16


def iota(shape, dim):
    return lax.broadcasted_iota(jnp.int32, shape, dim)


def pieces(v):
    hi = v.astype(bf16).astype(f32)
    rest = v - hi
    mid = rest.astype(bf16).astype(f32)
    return hi, mid, rest - mid


def params(collective_id=None, limit=40):
    if collective_id is None:
        return pltpu.CompilerParams(vmem_limit_bytes=limit << 20)
    return pltpu.CompilerParams(
        vmem_limit_bytes=limit << 20, collective_id=collective_id, has_side_effects=True
    )


def picker():
    return (iota((HALF, BLK), 1) % HALF == iota((HALF, BLK), 0)).astype(bf16)


def turn_over(pick, rows):
    return lax.dot_general(pick, rows, (((1,), (1,)), ((), ())), preferred_element_type=f32)


def fold(pick, tile):
    low = (iota((DIM, BLK), 1) < HALF).astype(bf16)
    rows = jnp.concatenate([tile * low, tile * (1.0 - low).astype(bf16)], axis=0)
    return turn_over(pick, rows).astype(bf16)


def fold_potential(pot, aug):
    lane = iota((HALF, BLK), 1)
    pick = picker()
    n = iota((8, 16, BLK), 1)
    h = iota((8, 16, BLK), 2) // HALF
    keep = ((n < 6) & (n // 3 == h)) | ((n >= 6) & (n < 9) & (h == 0))
    for g in range(8):
        hi, mid, lo = (v[:, None, :] for v in pieces(pot[8 * g : 8 * g + 8, :]))
        rows = jnp.where(
            n >= 6, 1.0, jnp.where(n % 3 == 0, hi, jnp.where(n % 3 == 1, mid, lo))
        )
        rows = jnp.where(keep, rows, 0.0).reshape(BLK, BLK).astype(bf16)
        turned = turn_over(pick, rows)
        for k in range(8):
            aug[8 * g + k] = jnp.where(lane // 16 == k, turned, 0.0).astype(bf16)
    n = iota((HALF, BLK), 1)
    aug[NBLK] = jnp.where((n == 0) | (n == 3), LOW, 0.0).astype(bf16)


def spread_rows(pot, rows):
    n = iota((8, 16, BLK), 1)
    for g in range(8):
        hi, mid, lo = (v[:, None, :] for v in pieces(pot[8 * g : 8 * g + 8, :]))
        v = jnp.where(n == 6, hi, jnp.where(n == 7, mid, jnp.where(n == 8, lo, 0.0)))
        rows[8 * g : 8 * g + 8] = v.astype(bf16)


def chunk_table(member):
    dot = functools.partial(jnp.dot, preferred_element_type=f32)
    m = member.astype(bf16)
    up = (iota((NBLK, NBLK), 0) < iota((NBLK, NBLK), 1)).astype(bf16)
    upto = (iota((NBLK, NBLK), 0) >= iota((NBLK, NBLK), 1)).astype(bf16)
    eye = (iota((NBLK, NBLK), 0) == iota((NBLK, NBLK), 1)).astype(bf16)
    place_of = (member * (dot(m, up) + 1.0)).astype(bf16)
    turned = turn_over(eye, place_of).astype(bf16)
    size = dot(m, jnp.ones((NBLK, LANES), bf16))
    many = jnp.floor((size + (CHUNK - 1.0)) * (1.0 / CHUNK))
    end = dot(upto, many.astype(bf16))
    row = iota((NBLK, LANES), 0).astype(f32)
    n = iota((NBLK, LANES), 1).astype(f32)
    before = (end <= n).astype(f32)
    p = jnp.sum(before, axis=0, keepdims=True)
    first = CHUNK * (n[:1] - jnp.sum(before * many, axis=0, keepdims=True))
    mine = dot(turned, (row == p).astype(bf16))
    rows = [
        NBLK + jnp.sum((row - NBLK) * (mine == first + (k + 1.0)).astype(f32), axis=0, keepdims=True)
        for k in range(CHUNK)
    ]
    rows += [p, end[NBLK - 1 :]] + [jnp.zeros((1, LANES), f32)] * (6 - CHUNK)
    return jnp.concatenate(rows, axis=0).astype(jnp.int32)


def sweep(table, lhs, aug, weights, pot_rows, process):
    n16 = iota((16, BLK), 0)
    left = (n16 < 3).astype(bf16)
    right = ((n16 >= 3) & (n16 < 6)).astype(bf16)
    zero = jnp.zeros((DIM, BLK), bf16)

    @pl.loop(0, (table[3, 0] + BODY - 1) // BODY)
    def _(turn):
        for k in range(BODY):
            n = BODY * turn + k
            p = table[2, n]
            safe = jnp.minimum(p, NBLK - 1)
            ids = [table[i, n] for i in range(CHUNK)]
            w = weights(safe)
            l16, r16 = left, right
            if pot_rows is not None:
                extra = pot_rows[safe]
                l16, r16 = left + extra, right + extra
            top = jnp.concatenate([w, zero], axis=1)
            mid = jnp.concatenate([zero, w], axis=1)
            low = jnp.concatenate([l16, r16], axis=1)
            rhs = jnp.concatenate([top, mid] + [low] * 8, axis=0)
            body = jnp.concatenate([lhs[jnp.minimum(q, NBLK - 1)] for q in ids], axis=0)
            tail = jnp.concatenate([aug[q] for q in ids], axis=0)
            both = jnp.concatenate([body, tail], axis=1)
            process(p, jnp.dot(both, rhs, preferred_element_type=f32))


def max_process(peak, total):
    def process(p, v):
        old, sums = peak[p], total[p]
        for k in range(CHUNK):
            u = v[k * HALF : (k + 1) * HALF].reshape(HALF // 8, 8, 2 * BLK)
            top = jnp.max(u, axis=0)
            new = jnp.maximum(old, jnp.maximum(top[:, :BLK], top[:, BLK:]))
            new2 = jnp.concatenate([new, new], axis=1)
            e = jnp.sum(jnp.exp2((u - new2[None]) * C2), axis=0)
            sums = sums * jnp.exp2((old - new) * C2) + (e[:, :BLK] + e[:, BLK:])
            old = new
        peak[p] = old
        total[p] = sums

    return process


def sum_process(total):
    def process(p, v):
        u = v.reshape(CHUNK * HALF // 8, 8, 2 * BLK)
        e = jnp.sum(jnp.exp2(u * C2), axis=0)
        total[p] = total[p] + (e[:, :BLK] + e[:, BLK:])

    return process


def init_peaks(peak, total):
    peak[...] = jnp.full(peak.shape, LOW, f32)
    total[...] = jnp.zeros(total.shape, f32)


def finish_peaks(peak, total):
    m = peak[0:NBLK]
    top = jnp.max(m, axis=1)
    s = jnp.sum(total[0:NBLK] * jnp.exp2((m - top[:, None, :]) * C2), axis=1)
    return top + jnp.log2(s) * (1.0 / C2)


def finish_total(total):
    return jnp.sum(total[0:NBLK], axis=1)


def x_weights(xt):
    return lambda p: xt[:, pl.ds(pl.multiple_of(p * BLK, BLK), BLK)]


def row1_kernel(table, b, yfold, xt, peak, total, aug):
    fold_potential(b, aug)
    init_peaks(peak, total)
    sweep(table, yfold, aug, x_weights(xt), None, max_process(peak, total))


def col1_kernel(table, a, xfold, yt, peak, total, aug):
    fold_potential(a, aug)
    init_peaks(peak, total)
    sweep(table, xfold, aug, lambda t: yt[t], None, max_process(peak, total))


def row2_kernel(table, rows, b, yfold, xt, total, aug):
    fold_potential(b, aug)
    total[...] = jnp.zeros(total.shape, f32)
    sweep(table, yfold, aug, x_weights(xt), rows, sum_process(total))


def col2_kernel(table, rows, a, xfold, yt, xsq, total, f_out, aug, f, sem):
    f[...] = a[...] * (1.0 / 32) + xsq[...] * (1.0 / 64)
    leave = pltpu.make_async_copy(f, f_out, sem.at[0])
    leave.start()
    fold_potential(a, aug)
    total[...] = jnp.zeros(total.shape, f32)
    sweep(table, xfold, aug, lambda t: yt[t], rows, sum_process(total))
    leave.wait()


AUG = pltpu.VMEM((NBLK + 1, HALF, BLK), bf16)
ROWS = jax.ShapeDtypeStruct((NBLK, 16, BLK), bf16)
ACC = jax.ShapeDtypeStruct((NBLK + 1, 8, BLK), f32)
TABLE = jax.ShapeDtypeStruct((8, LANES), jnp.int32)


def work_call(kernel, outs, *args, out_specs=None, scratch=()):
    return pl.pallas_call(
        kernel,
        out_shape=outs,
        in_specs=[SMEM] + [VMEM] * (len(args) - 1),
        out_specs=out_specs or jax.tree.map(lambda _: VMEM, outs),
        scratch_shapes=[AUG, *scratch],
        compiler_params=params(),
    )(*args)


def duals(n=NBLK):
    return jax.ShapeDtypeStruct((n, BLK), f32)


def place():
    i = lax.axis_index("src")
    core, z, y = lax.rem(i, 2), lax.rem(i // 2, NZ), i // (2 * NZ)
    return y, z, core


def at(y, z, core):
    return {"src": (y * NZ + z) * 2 + core}


def hail(devices):
    barrier = pltpu.get_barrier_semaphore()
    for d in devices:
        pl.semaphore_signal(barrier, inc=1, device_id=d, device_id_type=MESH)


def meet(devices):
    pl.semaphore_wait(pltpu.get_barrier_semaphore(), len(devices))


def send(src, dst, sends, recvs, k, device):
    copy = pltpu.make_async_remote_copy(
        src_ref=src, dst_ref=dst, send_sem=sends.at[k], recv_sem=recvs.at[k],
        device_id=device, device_id_type=MESH,
    )
    copy.start()
    return copy


def slot_of(dz):
    return 2 * dz - 1 if 0 < dz <= 4 else 2 * (NZ - dz) if dz else 0


GROUPS = ((0, 1), (1, 2), (3, 2), (5, 3))


def gather_kernel(
    own, bt_far, xt_far, yt, yfold, b0, row_table, col_table, xt, held, bt, ls, zs, zr, ys, yr, cs, cr
):
    y, z, core = place()
    pick = picker()
    z_devices = {k: at(y, lax.rem(z + k, NZ), core) for k in (4, 3, 5, 2, 6, 1, 7)}
    y_devices = {k: at(lax.rem(y + k, NY), z, core) for k in (2, 1, 3)}
    mate = at(y, z, 1 - core)
    everyone = list(z_devices.values()) + list(y_devices.values()) + [mate]
    mine = held.at[0, 0, 0]
    hail(everyone)
    here = [
        pltpu.make_async_copy(src, dst, ls.at[k])
        for k, (src, dst) in enumerate(((own, mine), (bt_far, bt), (xt_far, xt)))
    ]
    for c in here:
        c.start()
    here[0].wait()
    meet(everyone)

    z_copies = {}
    for k, d in z_devices.items():
        z_copies[k] = send(mine, held.at[0, 0, slot_of(NZ - k)], zs, zr, k - 1, d)
    y_copies = {}

    def on_y(g):
        first, size = GROUPS[g]
        for k, d in y_devices.items():
            part = held.at[0, 0, pl.ds(first, size)]
            dst = held.at[0, NY - k, pl.ds(first, size)]
            y_copies[k, g] = send(part, dst, ys, yr, 4 * (k - 1) + g, d)

    c_copies = []

    def on_mate(dy, dys, first, size):
        part = held.at[0, pl.ds(dy, dys), pl.ds(first, size)]
        dst = held.at[1, pl.ds(dy, dys), pl.ds(first, size)]
        c_copies.append(send(part, dst, cs, cr, len(c_copies), mate))

    def take(side, dy, s):
        back = lax.rem(s, 2)
        dz = back * ((s + 1) // 2) + (1 - back) * (NZ - s // 2)
        who = core if side == 0 else 1 - core
        t = (lax.rem(y + dy, NY) * NZ + lax.rem(z + dz, NZ)) * 2 + who
        tile = held[side, dy, s]
        yt[t] = tile
        yfold[t] = fold(pick, tile)
        wide = tile.astype(f32)
        b0[pl.ds(t, 1), :] = -0.5 * jnp.sum(wide * wide, axis=0, keepdims=True)

    def take_column(side):
        @pl.loop(0, NZ, step=4)
        def _(s):
            for i in range(4):
                take(side, 0, s + i)

    def take_group(side, g):
        @pl.loop(GROUPS[g][0], GROUPS[g][0] + GROUPS[g][1])
        def _(s):
            for dy in range(1, NY):
                take(side, dy, s)

    on_y(0)
    here[1].wait()
    here[2].wait()
    t = iota((NBLK, NBLK), 0)
    member = sum((bt[k : k + 1, :] == t).astype(f32) for k in range(SLOTS))
    col_table[...] = chunk_table(member)
    eye = (iota((NBLK, NBLK), 1) == t).astype(bf16)
    row_table[...] = chunk_table(turn_over(eye, member.astype(bf16)))
    for g, ks in ((1, (1, 7)), (2, (2, 6)), (3, (3, 5, 4))):
        for k in ks:
            z_copies[k].wait_recv()
        on_y(g)
    on_mate(0, 1, 0, NZ)
    for g in range(4):
        for k in (1, 3, 2):
            y_copies[k, g].wait_recv()
        on_mate(1, NY - 1, *GROUPS[g])
        if g == 0:
            take_column(0)
        take_group(0, g)
        if g == 1:
            c_copies[0].wait_recv()
            take_column(1)
        if g == 2:
            c_copies[1].wait_recv()
            take_group(1, 0)
    for g in range(1, 4):
        c_copies[1 + g].wait_recv()
        take_group(1, g)
    for c in list(z_copies.values()) + list(y_copies.values()) + c_copies:
        c.wait_send()


def gather(own, bt, xt):
    dma = pltpu.SemaphoreType.DMA
    blocks = jax.ShapeDtypeStruct((NBLK, DIM, BLK), bf16)
    return pl.pallas_call(
        gather_kernel,
        out_shape=(blocks, blocks, duals(), TABLE, TABLE, jax.ShapeDtypeStruct(xt.shape, bf16)),
        in_specs=[pl.BlockSpec(memory_space=pl.ANY)] * 3,
        out_specs=(VMEM,) * 6,
        scratch_shapes=[pltpu.VMEM((2, NY, NZ, DIM, BLK), bf16), pltpu.VMEM(bt.shape, jnp.int32)]
        + [dma((3,)), dma((7,)), dma((7,)), dma((12,)), dma((12,)), dma((5,)), dma((5,))],
        compiler_params=params(0, 50),
    )(own, bt, xt)


def spread(pairs, device_of, sends, recvs):
    for k, (src, dst) in enumerate(pairs):
        pltpu.make_async_remote_copy(
            src_ref=src, dst_ref=dst, send_sem=sends.at[0], recv_sem=recvs.at[0],
            device_id=device_of[k], device_id_type=MESH,
        ).start()


def collect(many, device, sends, recvs):
    pltpu.make_async_remote_copy(
        src_ref=many, dst_ref=many, send_sem=sends.at[0], recv_sem=recvs.at[0],
        device_id=device, device_id_type=MESH,
    ).wait()


def tgt_exchange(finish, meanwhile, mine, got, sends, recvs):
    me = lax.axis_index("tgt")
    devices = [{"tgt": lax.rem(me + k, NX)} for k in (2, 1, 3)]
    hail(devices)
    mine[...] = finish()
    meet(devices)
    spread([(mine, got.at[me])] * 3, devices, sends, recvs)
    got[me] = mine[...]
    meanwhile()
    collect(got.at[pl.ds(0, 3)], devices[0], sends, recvs)


def tgt1_kernel(peak, total, xt, a_ref, xfold, xsq, mine, got, sends, recvs):
    pick = picker()

    def fold_x():
        @pl.loop(0, NBLK, step=8)
        def _(p):
            for i in range(8):
                tile = xt[:, pl.ds(pl.multiple_of((p + i) * BLK, BLK), BLK)]
                xfold[p + i] = fold(pick, tile)
                wide = tile.astype(f32)
                xsq[pl.ds(p + i, 1), :] = jnp.sum(wide * wide, axis=0, keepdims=True)

    tgt_exchange(lambda: finish_peaks(peak, total), fold_x, mine, got, sends, recvs)
    a_ref[...] = -lse([got[k] for k in range(NX)]) - LOG_NS


def tgt2_kernel(total, old, b_ref, a_ref, rows, mine, got, sends, recvs):
    tgt_exchange(
        lambda: finish_total(total), lambda: spread_rows(b_ref, rows), mine, got, sends, recvs
    )
    s = (got[0] + got[1]) + (got[2] + got[3])
    a_ref[...] = old[...] - jnp.log2(s * NS) * (1.0 / C2)


def tgt_call(kernel, collective_id, outs, *args):
    dma = pltpu.SemaphoreType.DMA
    mine = pltpu.VMEM((NBLK, BLK), f32)
    return pl.pallas_call(
        kernel,
        out_shape=outs,
        in_specs=[VMEM] * len(args),
        out_specs=jax.tree.map(lambda _: VMEM, outs),
        scratch_shapes=[mine, pltpu.VMEM((NX, NBLK, BLK), f32), dma((1,)), dma((1,))],
        compiler_params=params(collective_id),
    )(*args)


def lse(parts):
    top = functools.reduce(jnp.maximum, parts)
    s = sum(jnp.exp2((v - top) * C2) for v in parts)
    return top + jnp.log2(s) * (1.0 / C2)


def mates():
    y, z, core = place()
    m = y * 2 + core

    def side(k):
        other = lax.rem(m + k, 8)
        return other, at(other // 2, z, lax.rem(other, 2))

    def up(k):
        other = lax.rem(z + k, NZ)
        return other, at(y, other, core)

    return m, z, [side(k) for k in range(1, 8)], [up(k) for k in (4, 3, 5, 2, 6, 1, 7)]


def rows_of(k):
    return pl.ds((k // 2) * 2 * NZ + k % 2, NZ, stride=2)


def scatter_sides(finish, combine, m, sides, ups, mine, order, r1, sends, recvs):
    devices = [d for _, d in ups + sides]
    hail(devices)
    mine[...] = finish()
    for k in range(8):
        order[k] = mine[rows_of(k), :]
    meet(devices)
    spread([(order.at[o], r1.at[m]) for o, _ in sides], [d for _, d in sides], sends, recvs)
    r1[m] = order[m]
    collect(r1.at[pl.ds(0, 7)], sides[0][1], sends, recvs)
    return combine([r1[k] for k in range(8)])


def src1_kernel(peak, total, a_ref, b_ref, own_ref, a_rows, mine, order, r1, tile, r2, done, r4, s1, q1, s2, q2, s3, q3):
    m, z, sides, ups = mates()
    tile[...] = scatter_sides(
        lambda: finish_peaks(peak, total), lse, m, sides, ups, mine, order, r1, s1, q1
    )
    spread([(tile, r2.at[z])] * 7, [d for _, d in ups], s2, q2)
    r2[z] = tile[...]
    spread_rows(a_ref, a_rows)
    collect(r2.at[pl.ds(0, 7)], ups[0][1], s2, q2)
    done[...] = -lse([r2[k] for k in range(8)]) - LOG_NT
    spread([(done, r4.at[m])] * 7, [d for _, d in sides], s3, q3)
    r4[m] = done[...]
    own_ref[...] = jnp.broadcast_to(done[pl.ds(z, 1), :], (8, BLK))
    collect(r4.at[pl.ds(0, 7)], sides[0][1], s3, q3)
    for k in range(8):
        b_ref[rows_of(k), :] = r4[k]


def src2_kernel(total, old, yt_ref, g_ref, mine, order, r1, rows, r2, s1, q1, s2, q2):
    m, z, sides, ups = mates()
    first = scatter_sides(
        lambda: finish_total(total), sum, m, sides, ups, mine, order, r1, s1, q1
    )
    for k in range(8):
        rows[k] = jnp.broadcast_to(first[k : k + 1], (8, BLK))
    spread([(rows.at[o], r2.at[z]) for o, _ in ups], [d for _, d in ups], s2, q2)
    r2[z] = rows[z]
    y = yt_ref[...].astype(f32)
    sq = jnp.sum(y * y, axis=0, keepdims=True)
    collect(r2.at[pl.ds(0, 7)], ups[0][1], s2, q2)
    s = sum([r2[k] for k in range(8)])
    b = old[...] - jnp.log2(s * NT) * (1.0 / C2)
    g_ref[...] = b * (1.0 / 32) + sq * (1.0 / 64)


def src_call(kernel, collective_id, outs, scratch, phases, *args):
    mine = pltpu.VMEM((NBLK, BLK), f32)
    return pl.pallas_call(
        kernel,
        out_shape=outs,
        in_specs=[VMEM] * len(args),
        out_specs=jax.tree.map(lambda _: VMEM, outs),
        scratch_shapes=[mine] + scratch + [pltpu.SemaphoreType.DMA((1,))] * (2 * phases),
        compiler_params=params(collective_id),
    )(*args)


def local(source_features, target_features, block_targets):
    own_yt = target_features[0].T
    block, tile = pltpu.VMEM((8, 8, BLK), f32), pltpu.VMEM((8, BLK), f32)

    blocks = jax.ShapeDtypeStruct((NBLK, DIM, BLK), bf16)
    yt, yfold, b0, row_table, col_table, xt = gather(
        own_yt, block_targets[:, 0, :].T, source_features.T
    )
    peak, total = work_call(row1_kernel, (ACC, ACC), row_table, b0, yfold, xt)
    a, xfold, xsq = tgt_call(tgt1_kernel, 1, (duals(), blocks, duals()), peak, total, xt)
    peak, total = work_call(col1_kernel, (ACC, ACC), col_table, a, xfold, yt)
    b, own, rows = src_call(
        src1_kernel, 2, (duals(), duals(8), ROWS), [block, block, tile, block, tile, block], 3,
        peak, total, a,
    )
    total = work_call(row2_kernel, ACC, row_table, rows, b, yfold, xt)
    a, rows = tgt_call(tgt2_kernel, 3, (duals(), ROWS), total, a, b)
    total, f = work_call(
        col2_kernel, (ACC, duals()), col_table, rows, a, xfold, yt, xsq,
        out_specs=(VMEM, pl.BlockSpec(memory_space=pl.ANY)),
        scratch=(pltpu.VMEM((NBLK, BLK), f32), pltpu.SemaphoreType.DMA((1,))),
    )
    g = src_call(src2_kernel, 4, duals(8), [block] * 4, 2, total, own, own_yt)
    return f.reshape(-1), g[0:1]


def solution(mesh):
    in_specs = (P("src", None), P("tgt", "src", None), P("src", "tgt", None))
    out_specs = (P("src"), P("tgt", "src"))
    return jax.shard_map(local, mesh=mesh, in_specs=in_specs, out_specs=out_specs, check_vma=False)
```

```python
import functools
import math

import jax
import jax.numpy as jnp
from jax import lax
from jax.experimental import pallas as pl
from jax.experimental.pallas import tpu as pltpu
from jax.sharding import PartitionSpec as P

BLK = 128
DIM = 64
HALF = BLK // 2
NBLK = 64
SLOTS = 8
CHUNK = 2
LANES = 384
EPSILON = 0.01
NS = 524288
NT = 32768
NY, NZ, NX = 4, 8, 4
RATE = 2.0 / (DIM * EPSILON)
C2 = RATE / math.log(2.0)
LOG_NS = math.log(NS) / RATE
LOG_NT = math.log(NT) / RATE
LOW = -1.0e30
BODY = 96
MESH = pl.DeviceIdType.MESH
VMEM = pl.BlockSpec(memory_space=pltpu.VMEM)
f32, bf16 = jnp.float32, jnp.bfloat16


def iota(shape, dim):
    return lax.broadcasted_iota(jnp.int32, shape, dim)


def pieces(v):
    hi = v.astype(bf16).astype(f32)
    rest = v - hi
    mid = rest.astype(bf16).astype(f32)
    return hi, mid, rest - mid


def params(collective_id=None, limit=40):
    if collective_id is None:
        return pltpu.CompilerParams(vmem_limit_bytes=limit << 20)
    return pltpu.CompilerParams(
        vmem_limit_bytes=limit << 20, collective_id=collective_id, has_side_effects=True
    )


def picker():
    return (iota((HALF, BLK), 1) % HALF == iota((HALF, BLK), 0)).astype(bf16)


def turn_over(pick, rows):
    return lax.dot_general(pick, rows, (((1,), (1,)), ((), ())), preferred_element_type=f32)


def fold(pick, tile):
    low = (iota((DIM, BLK), 1) < HALF).astype(bf16)
    rows = jnp.concatenate([tile * low, tile * (1.0 - low).astype(bf16)], axis=0)
    return turn_over(pick, rows).astype(bf16)


def fold_potential(pot, aug):
    lane = iota((HALF, BLK), 1)
    pick = picker()
    n = iota((8, 16, BLK), 1)
    h = iota((8, 16, BLK), 2) // HALF
    keep = ((n < 6) & (n // 3 == h)) | ((n >= 6) & (n < 9) & (h == 0))
    for g in range(8):
        hi, mid, lo = (v[:, None, :] for v in pieces(pot[8 * g : 8 * g + 8, :]))
        rows = jnp.where(
            n >= 6, 1.0, jnp.where(n % 3 == 0, hi, jnp.where(n % 3 == 1, mid, lo))
        )
        rows = jnp.where(keep, rows, 0.0).reshape(BLK, BLK).astype(bf16)
        turned = turn_over(pick, rows)
        for k in range(8):
            aug[8 * g + k] = jnp.where(lane // 16 == k, turned, 0.0).astype(bf16)
    n = iota((HALF, BLK), 1)
    aug[NBLK] = jnp.where((n == 0) | (n == 3), LOW, 0.0).astype(bf16)


def spread_rows(pot, rows):
    n = iota((8, 16, BLK), 1)
    for g in range(8):
        hi, mid, lo = (v[:, None, :] for v in pieces(pot[8 * g : 8 * g + 8, :]))
        v = jnp.where(n == 6, hi, jnp.where(n == 7, mid, jnp.where(n == 8, lo, 0.0)))
        rows[8 * g : 8 * g + 8] = v.astype(bf16)


def chunk_table(member):
    dot = functools.partial(jnp.dot, preferred_element_type=f32)
    m = member.astype(bf16)
    up = (iota((NBLK, NBLK), 0) < iota((NBLK, NBLK), 1)).astype(bf16)
    upto = (iota((NBLK, NBLK), 0) >= iota((NBLK, NBLK), 1)).astype(bf16)
    eye = (iota((NBLK, NBLK), 0) == iota((NBLK, NBLK), 1)).astype(bf16)
    place_of = (member * (dot(m, up) + 1.0)).astype(bf16)
    turned = turn_over(eye, place_of).astype(bf16)
    size = dot(m, jnp.ones((NBLK, LANES), bf16))
    many = jnp.floor((size + (CHUNK - 1.0)) * (1.0 / CHUNK))
    end = dot(upto, many.astype(bf16))
    row = iota((NBLK, LANES), 0).astype(f32)
    n = iota((NBLK, LANES), 1).astype(f32)
    before = (end <= n).astype(f32)
    p = jnp.sum(before, axis=0, keepdims=True)
    first = CHUNK * (n[:1] - jnp.sum(before * many, axis=0, keepdims=True))
    mine = dot(turned, (row == p).astype(bf16))
    rows = [
        NBLK + jnp.sum((row - NBLK) * (mine == first + (k + 1.0)).astype(f32), axis=0, keepdims=True)
        for k in range(CHUNK)
    ]
    word = p + BLK * (rows[0] + BLK * rows[1])
    return jnp.where(n[:1] == LANES - 1, end[NBLK - 1 :], word).astype(jnp.int32)


def sweep(table, lhs, aug, weights, pot_rows, process):
    n16 = iota((16, BLK), 0)
    left = (n16 < 3).astype(bf16)
    right = ((n16 >= 3) & (n16 < 6)).astype(bf16)
    zero = jnp.zeros((DIM, BLK), bf16)

    @pl.loop(0, (table[0, LANES - 1] + BODY - 1) // BODY)
    def _(turn):
        for k in range(BODY):
            word = table[0, BODY * turn + k]
            p = word & (BLK - 1)
            safe = jnp.minimum(p, NBLK - 1)
            ids = [(word >> 7) & (BLK - 1), word >> 14]
            w = weights(safe)
            l16, r16 = left, right
            if pot_rows is not None:
                extra = pot_rows[safe]
                l16, r16 = left + extra, right + extra
            top = jnp.concatenate([w, zero], axis=1)
            mid = jnp.concatenate([zero, w], axis=1)
            low = jnp.concatenate([l16, r16], axis=1)
            rhs = jnp.concatenate([top, mid] + [low] * 8, axis=0)
            body = jnp.concatenate([lhs[jnp.minimum(q, NBLK - 1)] for q in ids], axis=0)
            tail = jnp.concatenate([aug[q] for q in ids], axis=0)
            both = jnp.concatenate([body, tail], axis=1)
            process(p, jnp.dot(both, rhs, preferred_element_type=f32))


def max_process(peak, total):
    def process(p, v):
        old, sums = peak[p], total[p]
        for k in range(CHUNK):
            u = v[k * HALF : (k + 1) * HALF].reshape(HALF // 8, 8, 2 * BLK)
            top = jnp.max(u, axis=0)
            new = jnp.maximum(old, jnp.maximum(top[:, :BLK], top[:, BLK:]))
            new2 = jnp.concatenate([new, new], axis=1)
            e = jnp.sum(jnp.exp2((u - new2[None]) * C2), axis=0)
            sums = sums * jnp.exp2((old - new) * C2) + (e[:, :BLK] + e[:, BLK:])
            old = new
        peak[p] = old
        total[p] = sums

    return process


def sum_process(total):
    def process(p, v):
        u = v.reshape(CHUNK * HALF // 8, 8, 2 * BLK)
        e = jnp.sum(jnp.exp2(u * C2), axis=0)
        total[p] = total[p] + (e[:, :BLK] + e[:, BLK:])

    return process


def init_peaks(peak, total):
    peak[...] = jnp.full(peak.shape, LOW, f32)
    total[...] = jnp.zeros(total.shape, f32)


def finish_peaks(peak, total):
    m = peak[0:NBLK]
    top = jnp.max(m, axis=1)
    s = jnp.sum(total[0:NBLK] * jnp.exp2((m - top[:, None, :]) * C2), axis=1)
    return top + jnp.log2(s) * (1.0 / C2)


def finish_total(total):
    return jnp.sum(total[0:NBLK], axis=1)


def x_weights(xt):
    return lambda p: xt[:, pl.ds(pl.multiple_of(p * BLK, BLK), BLK)]


def fetch(far, table, sem):
    copy = pltpu.make_async_copy(far, table, sem.at[0])
    copy.start()
    return copy


def row1_kernel(far, b, yfold, xt, peak, total, aug, table, sem):
    listed = fetch(far, table, sem)
    fold_potential(b, aug)
    init_peaks(peak, total)
    listed.wait()
    sweep(table, yfold, aug, x_weights(xt), None, max_process(peak, total))


def col1_kernel(far, a, xfold, yt, peak, total, aug, table, sem):
    listed = fetch(far, table, sem)
    fold_potential(a, aug)
    init_peaks(peak, total)
    listed.wait()
    sweep(table, xfold, aug, lambda t: yt[t], None, max_process(peak, total))


def row2_kernel(far, rows, b, yfold, xt, total, aug, table, sem):
    listed = fetch(far, table, sem)
    fold_potential(b, aug)
    total[...] = jnp.zeros(total.shape, f32)
    listed.wait()
    sweep(table, yfold, aug, x_weights(xt), rows, sum_process(total))


def col2_kernel(far, rows, a, xfold, yt, xsq, total, f_out, aug, table, sem, f, f_sem):
    listed = fetch(far, table, sem)
    f[...] = a[...] * (1.0 / 32) + xsq[...] * (1.0 / 64)
    leave = pltpu.make_async_copy(f, f_out, f_sem.at[0])
    leave.start()
    fold_potential(a, aug)
    total[...] = jnp.zeros(total.shape, f32)
    listed.wait()
    sweep(table, xfold, aug, lambda t: yt[t], rows, sum_process(total))
    leave.wait()


AUG = pltpu.VMEM((NBLK + 1, HALF, BLK), bf16)
ROWS = jax.ShapeDtypeStruct((NBLK, 16, BLK), bf16)
ACC = jax.ShapeDtypeStruct((NBLK + 1, 8, BLK), f32)
TABLE = jax.ShapeDtypeStruct((1, LANES), jnp.int32)


def work_call(kernel, outs, *args, out_specs=None, scratch=()):
    return pl.pallas_call(
        kernel,
        out_shape=outs,
        in_specs=[VMEM] * len(args),
        out_specs=out_specs or jax.tree.map(lambda _: VMEM, outs),
        scratch_shapes=[AUG, pltpu.SMEM(TABLE.shape, TABLE.dtype), pltpu.SemaphoreType.DMA((1,)), *scratch],
        compiler_params=params(),
    )(*args)


def duals(n=NBLK):
    return jax.ShapeDtypeStruct((n, BLK), f32)


def place():
    i = lax.axis_index("src")
    core, z, y = lax.rem(i, 2), lax.rem(i // 2, NZ), i // (2 * NZ)
    return y, z, core


def at(y, z, core):
    return {"src": (y * NZ + z) * 2 + core}


def hail(devices):
    barrier = pltpu.get_barrier_semaphore()
    for d in devices:
        pl.semaphore_signal(barrier, inc=1, device_id=d, device_id_type=MESH)


def meet(devices):
    pl.semaphore_wait(pltpu.get_barrier_semaphore(), len(devices))


def send(src, dst, sends, recvs, k, device):
    copy = pltpu.make_async_remote_copy(
        src_ref=src, dst_ref=dst, send_sem=sends.at[k], recv_sem=recvs.at[k],
        device_id=device, device_id_type=MESH,
    )
    copy.start()
    return copy


def slot_of(dz):
    return 2 * dz - 1 if 0 < dz <= 4 else 2 * (NZ - dz) if dz else 0


GROUPS = ((0, 1), (1, 2), (3, 2), (5, 3))


def gather_kernel(
    packed, xt_far, yt, yfold, b0, row_table, col_table, xt, held, ls, zs, zr, ys, yr, cs, cr
):
    y, z, core = place()
    pick = picker()
    z_devices = {k: at(y, lax.rem(z + k, NZ), core) for k in (4, 3, 5, 2, 6, 1, 7)}
    y_devices = {k: at(lax.rem(y + k, NY), z, core) for k in (2, 1, 3)}
    mate = at(y, z, 1 - core)
    everyone = list(z_devices.values()) + list(y_devices.values()) + [mate]
    mine = held.at[0, 0, 0]
    hail(everyone)
    here = pltpu.make_async_copy(xt_far, xt, ls.at[0])
    here.start()
    mine[...] = packed[0:DIM, :]
    meet(everyone)

    z_copies = {}
    for k, d in z_devices.items():
        z_copies[k] = send(mine, held.at[0, 0, slot_of(NZ - k)], zs, zr, k - 1, d)
    y_copies = {}

    def on_y(g):
        first, size = GROUPS[g]
        for k, d in y_devices.items():
            part = held.at[0, 0, pl.ds(first, size)]
            dst = held.at[0, NY - k, pl.ds(first, size)]
            y_copies[k, g] = send(part, dst, ys, yr, 4 * (k - 1) + g, d)

    c_copies = []

    def on_mate(dy, dys, first, size):
        part = held.at[0, pl.ds(dy, dys), pl.ds(first, size)]
        dst = held.at[1, pl.ds(dy, dys), pl.ds(first, size)]
        c_copies.append(send(part, dst, cs, cr, len(c_copies), mate))

    def take(side, dy, s):
        back = lax.rem(s, 2)
        dz = back * ((s + 1) // 2) + (1 - back) * (NZ - s // 2)
        who = core if side == 0 else 1 - core
        t = (lax.rem(y + dy, NY) * NZ + lax.rem(z + dz, NZ)) * 2 + who
        tile = held[side, dy, s]
        yt[t] = tile
        yfold[t] = fold(pick, tile)
        wide = tile.astype(f32)
        b0[pl.ds(t, 1), :] = -0.5 * jnp.sum(wide * wide, axis=0, keepdims=True)

    def take_column(side):
        @pl.loop(0, NZ, step=4)
        def _(s):
            for i in range(4):
                take(side, 0, s + i)

    def take_group(side, g):
        @pl.loop(GROUPS[g][0], GROUPS[g][0] + GROUPS[g][1])
        def _(s):
            for dy in range(1, NY):
                take(side, dy, s)

    on_y(0)
    t = iota((NBLK, NBLK), 0)
    bt = packed[DIM:, 0:NBLK].astype(f32)
    member = sum((bt[k : k + 1, :] == t.astype(f32)).astype(f32) for k in range(SLOTS))
    col_table[...] = chunk_table(member)
    eye = (iota((NBLK, NBLK), 1) == t).astype(bf16)
    row_table[...] = chunk_table(turn_over(eye, member.astype(bf16)))
    for g, ks in ((1, (1, 7)), (2, (2, 6)), (3, (3, 5, 4))):
        for k in ks:
            z_copies[k].wait_recv()
        on_y(g)
    on_mate(0, 1, 0, NZ)
    for g in range(4):
        for k in (1, 3, 2):
            y_copies[k, g].wait_recv()
        on_mate(1, NY - 1, *GROUPS[g])
        if g == 0:
            take_column(0)
        take_group(0, g)
        if g == 1:
            c_copies[0].wait_recv()
            take_column(1)
        if g == 2:
            c_copies[1].wait_recv()
            take_group(1, 0)
    for g in range(1, 4):
        c_copies[1 + g].wait_recv()
        take_group(1, g)
    here.wait()
    for c in list(z_copies.values()) + list(y_copies.values()) + c_copies:
        c.wait_send()


def gather(packed, xt):
    dma = pltpu.SemaphoreType.DMA
    blocks = jax.ShapeDtypeStruct((NBLK, DIM, BLK), bf16)
    return pl.pallas_call(
        gather_kernel,
        out_shape=(blocks, blocks, duals(), TABLE, TABLE, jax.ShapeDtypeStruct(xt.shape, bf16)),
        in_specs=[VMEM, pl.BlockSpec(memory_space=pl.ANY)],
        out_specs=(VMEM,) * 6,
        scratch_shapes=[pltpu.VMEM((2, NY, NZ, DIM, BLK), bf16)]
        + [dma((1,)), dma((7,)), dma((7,)), dma((12,)), dma((12,)), dma((5,)), dma((5,))],
        compiler_params=params(0, 50),
    )(packed, xt)


def spread(pairs, device_of, sends, recvs):
    for k, (src, dst) in enumerate(pairs):
        pltpu.make_async_remote_copy(
            src_ref=src, dst_ref=dst, send_sem=sends.at[0], recv_sem=recvs.at[0],
            device_id=device_of[k], device_id_type=MESH,
        ).start()


def collect(many, device, sends, recvs):
    pltpu.make_async_remote_copy(
        src_ref=many, dst_ref=many, send_sem=sends.at[0], recv_sem=recvs.at[0],
        device_id=device, device_id_type=MESH,
    ).wait()


def tgt_exchange(finish, meanwhile, mine, got, sends, recvs):
    me = lax.axis_index("tgt")
    devices = [{"tgt": lax.rem(me + k, NX)} for k in (2, 1, 3)]
    hail(devices)
    mine[...] = finish().astype(mine.dtype)
    meet(devices)
    spread([(mine, got.at[me])] * 3, devices, sends, recvs)
    got[me] = mine[...]
    meanwhile()
    collect(got.at[pl.ds(0, 3)], devices[0], sends, recvs)


def tgt1_kernel(peak, total, xt, a_ref, xfold, xsq, mine, got, sends, recvs):
    pick = picker()

    def fold_x():
        @pl.loop(0, NBLK, step=8)
        def _(p):
            for i in range(8):
                tile = xt[:, pl.ds(pl.multiple_of((p + i) * BLK, BLK), BLK)]
                xfold[p + i] = fold(pick, tile)
                wide = tile.astype(f32)
                xsq[pl.ds(p + i, 1), :] = jnp.sum(wide * wide, axis=0, keepdims=True)

    tgt_exchange(lambda: finish_peaks(peak, total), fold_x, mine, got, sends, recvs)
    a_ref[...] = -lse([got[k] for k in range(NX)]) - LOG_NS


def tgt2_kernel(total, old, b_ref, a_ref, rows, mine, got, sends, recvs):
    tgt_exchange(
        lambda: finish_total(total), lambda: spread_rows(b_ref, rows), mine, got, sends, recvs
    )
    g0, g1, g2, g3 = (got[k].astype(f32) for k in range(NX))
    s = (g0 + g1) + (g2 + g3)
    a_ref[...] = old[...] - jnp.log2(s * NS) * (1.0 / C2)


def tgt_call(kernel, collective_id, kind, outs, *args):
    dma = pltpu.SemaphoreType.DMA
    mine = pltpu.VMEM((NBLK, BLK), kind)
    return pl.pallas_call(
        kernel,
        out_shape=outs,
        in_specs=[VMEM] * len(args),
        out_specs=jax.tree.map(lambda _: VMEM, outs),
        scratch_shapes=[mine, pltpu.VMEM((NX, NBLK, BLK), kind), dma((1,)), dma((1,))],
        compiler_params=params(collective_id),
    )(*args)


def lse(parts):
    top = functools.reduce(jnp.maximum, parts)
    s = sum(jnp.exp2((v - top) * C2) for v in parts)
    return top + jnp.log2(s) * (1.0 / C2)


def mates():
    y, z, core = place()
    m = y * 2 + core

    def side(k):
        other = lax.rem(m + k, 8)
        return other, at(other // 2, z, lax.rem(other, 2))

    def up(k):
        other = lax.rem(z + k, NZ)
        return other, at(y, other, core)

    far_first = (4, 3, 5, 2, 6, 1, 7)
    return m, z, [side(k) for k in far_first], [up(k) for k in far_first]


def rows_of(k):
    return pl.ds((k // 2) * 2 * NZ + k % 2, NZ, stride=2)


def scatter_sides(finish, combine, m, sides, ups, mine, order, r1, sends, recvs):
    devices = [d for _, d in ups + sides]
    hail(devices)
    mine[...] = finish()
    for k in range(8):
        order[k] = mine[rows_of(k), :]
    meet(devices)
    spread([(order.at[o], r1.at[m]) for o, _ in sides], [d for _, d in sides], sends, recvs)
    r1[m] = order[m]
    collect(r1.at[pl.ds(0, 7)], sides[0][1], sends, recvs)
    return combine([r1[k] for k in range(8)])


def src1_kernel(peak, total, a_ref, b_ref, own_ref, a_rows, mine, order, r1, tile, r2, done, r4, s1, q1, s2, q2, s3, q3):
    m, z, sides, ups = mates()
    tile[...] = scatter_sides(
        lambda: finish_peaks(peak, total), lse, m, sides, ups, mine, order, r1, s1, q1
    )
    spread([(tile, r2.at[z])] * 7, [d for _, d in ups], s2, q2)
    r2[z] = tile[...]
    spread_rows(a_ref, a_rows)
    collect(r2.at[pl.ds(0, 7)], ups[0][1], s2, q2)
    done[...] = -lse([r2[k] for k in range(8)]) - LOG_NT
    spread([(done, r4.at[m])] * 7, [d for _, d in sides], s3, q3)
    r4[m] = done[...]
    own_ref[...] = jnp.broadcast_to(done[pl.ds(z, 1), :], (8, BLK))
    collect(r4.at[pl.ds(0, 7)], sides[0][1], s3, q3)
    for k in range(8):
        b_ref[rows_of(k), :] = r4[k]


def src2_kernel(total, old, yt_ref, g_ref, mine, order, r1, rows, r2, s1, q1, s2, q2):
    m, z, sides, ups = mates()
    first = scatter_sides(
        lambda: finish_total(total), sum, m, sides, ups, mine, order, r1, s1, q1
    )
    for k in range(8):
        rows[k] = jnp.broadcast_to(first[k : k + 1], (8, BLK))
    spread([(rows.at[o], r2.at[z]) for o, _ in ups], [d for _, d in ups], s2, q2)
    r2[z] = rows[z]
    y = yt_ref[...].astype(f32)
    sq = jnp.sum(y * y, axis=0, keepdims=True)
    collect(r2.at[pl.ds(0, 7)], ups[0][1], s2, q2)
    s = sum([r2[k] for k in range(8)])
    b = old[...] - jnp.log2(s * NT) * (1.0 / C2)
    g_ref[...] = b * (1.0 / 32) + sq * (1.0 / 64)


def src_call(kernel, collective_id, outs, scratch, phases, *args):
    mine = pltpu.VMEM((NBLK, BLK), f32)
    return pl.pallas_call(
        kernel,
        out_shape=outs,
        in_specs=[VMEM] * len(args),
        out_specs=jax.tree.map(lambda _: VMEM, outs),
        scratch_shapes=[mine] + scratch + [pltpu.SemaphoreType.DMA((1,))] * (2 * phases),
        compiler_params=params(collective_id),
    )(*args)


def local(source_features, target_features, block_targets):
    own_yt = target_features[0].T
    block, tile = pltpu.VMEM((8, 8, BLK), f32), pltpu.VMEM((8, BLK), f32)

    blocks = jax.ShapeDtypeStruct((NBLK, DIM, BLK), bf16)
    listed = block_targets[:, 0, :].T.astype(bf16)
    packed = jnp.concatenate([own_yt, jnp.pad(listed, ((0, 8), (0, BLK - NBLK)))], axis=0)
    yt, yfold, b0, row_table, col_table, xt = gather(packed, source_features.T)
    peak, total = work_call(row1_kernel, (ACC, ACC), row_table, b0, yfold, xt)
    a, xfold, xsq = tgt_call(tgt1_kernel, 1, f32, (duals(), blocks, duals()), peak, total, xt)
    peak, total = work_call(col1_kernel, (ACC, ACC), col_table, a, xfold, yt)
    b, own, rows = src_call(
        src1_kernel, 2, (duals(), duals(8), ROWS), [block, block, tile, block, tile, block], 3,
        peak, total, a,
    )
    total = work_call(row2_kernel, ACC, row_table, rows, b, yfold, xt)
    a, rows = tgt_call(tgt2_kernel, 3, bf16, (duals(), ROWS), total, a, b)
    total, f = work_call(
        col2_kernel, (ACC, duals()), col_table, rows, a, xfold, yt, xsq,
        out_specs=(VMEM, pl.BlockSpec(memory_space=pl.ANY)),
        scratch=(pltpu.VMEM((NBLK, BLK), f32), pltpu.SemaphoreType.DMA((1,))),
    )
    g = src_call(src2_kernel, 4, duals(8), [block] * 4, 2, total, own, own_yt)
    return f.reshape(-1), g[0:1]


def solution(mesh):
    in_specs = (P("src", None), P("tgt", "src", None), P("src", "tgt", None))
    out_specs = (P("src"), P("tgt", "src"))
    return jax.shard_map(local, mesh=mesh, in_specs=in_specs, out_specs=out_specs, check_vma=False)
```

```python
import functools
import math

import jax
import jax.numpy as jnp
from jax import lax
from jax.experimental import pallas as pl
from jax.experimental.pallas import tpu as pltpu
from jax.sharding import PartitionSpec as P

BLK = 128
DIM = 64
HALF = BLK // 2
NBLK = 64
SLOTS = 8
CHUNK = 2
LANES = 384
EPSILON = 0.01
NS = 524288
NT = 32768
NY, NZ, NX = 4, 8, 4
RATE = 2.0 / (DIM * EPSILON)
C2 = RATE / math.log(2.0)
LOG_NS = math.log(NS) / RATE
LOG_NT = math.log(NT) / RATE
LOW = -1.0e30
BODY = 96
MESH = pl.DeviceIdType.MESH
VMEM = pl.BlockSpec(memory_space=pltpu.VMEM)
f32, bf16 = jnp.float32, jnp.bfloat16


def iota(shape, dim):
    return lax.broadcasted_iota(jnp.int32, shape, dim)


def pieces(v):
    hi = v.astype(bf16).astype(f32)
    rest = v - hi
    mid = rest.astype(bf16).astype(f32)
    return hi, mid, rest - mid


def params(collective_id=None, limit=40):
    if collective_id is None:
        return pltpu.CompilerParams(vmem_limit_bytes=limit << 20)
    return pltpu.CompilerParams(
        vmem_limit_bytes=limit << 20, collective_id=collective_id, has_side_effects=True
    )


def picker():
    return (iota((HALF, BLK), 1) % HALF == iota((HALF, BLK), 0)).astype(bf16)


def turn_over(pick, rows):
    return lax.dot_general(pick, rows, (((1,), (1,)), ((), ())), preferred_element_type=f32)


def fold(pick, tile):
    low = (iota((DIM, BLK), 1) < HALF).astype(bf16)
    rows = jnp.concatenate([tile * low, tile * (1.0 - low).astype(bf16)], axis=0)
    return turn_over(pick, rows).astype(bf16)


def fold_potential(pot, aug):
    lane = iota((HALF, BLK), 1)
    pick = picker()
    n = iota((8, 16, BLK), 1)
    h = iota((8, 16, BLK), 2) // HALF
    keep = ((n < 6) & (n // 3 == h)) | ((n >= 6) & (n < 9) & (h == 0))
    for g in range(8):
        hi, mid, lo = (v[:, None, :] for v in pieces(pot[8 * g : 8 * g + 8, :]))
        rows = jnp.where(
            n >= 6, 1.0, jnp.where(n % 3 == 0, hi, jnp.where(n % 3 == 1, mid, lo))
        )
        rows = jnp.where(keep, rows, 0.0).reshape(BLK, BLK).astype(bf16)
        turned = turn_over(pick, rows)
        for k in range(8):
            aug[8 * g + k] = jnp.where(lane // 16 == k, turned, 0.0).astype(bf16)
    n = iota((HALF, BLK), 1)
    aug[NBLK] = jnp.where((n == 0) | (n == 3), LOW, 0.0).astype(bf16)


def spread_rows(pot, rows):
    n = iota((8, 16, BLK), 1)
    for g in range(8):
        hi, mid, lo = (v[:, None, :] for v in pieces(pot[8 * g : 8 * g + 8, :]))
        v = jnp.where(n == 6, hi, jnp.where(n == 7, mid, jnp.where(n == 8, lo, 0.0)))
        rows[8 * g : 8 * g + 8] = v.astype(bf16)


def chunk_table(member):
    dot = functools.partial(jnp.dot, preferred_element_type=f32)
    m = member.astype(bf16)
    up = (iota((NBLK, NBLK), 0) < iota((NBLK, NBLK), 1)).astype(bf16)
    upto = (iota((NBLK, NBLK), 0) >= iota((NBLK, NBLK), 1)).astype(bf16)
    eye = (iota((NBLK, NBLK), 0) == iota((NBLK, NBLK), 1)).astype(bf16)
    place_of = (member * (dot(m, up) + 1.0)).astype(bf16)
    turned = turn_over(eye, place_of).astype(bf16)
    size = dot(m, jnp.ones((NBLK, LANES), bf16))
    many = jnp.floor((size + (CHUNK - 1.0)) * (1.0 / CHUNK))
    end = dot(upto, many.astype(bf16))
    row = iota((NBLK, LANES), 0).astype(f32)
    n = iota((NBLK, LANES), 1).astype(f32)
    before = (end <= n).astype(f32)
    p = jnp.sum(before, axis=0, keepdims=True)
    first = CHUNK * (n[:1] - jnp.sum(before * many, axis=0, keepdims=True))
    mine = dot(turned, (row == p).astype(bf16))
    rows = [
        NBLK + jnp.sum((row - NBLK) * (mine == first + (k + 1.0)).astype(f32), axis=0, keepdims=True)
        for k in range(CHUNK)
    ]
    word = p + BLK * (rows[0] + BLK * rows[1])
    return jnp.where(n[:1] == LANES - 1, end[NBLK - 1 :], word).astype(jnp.int32)


def sweep(table, lhs, aug, weights, pot_rows, process):
    n16 = iota((16, BLK), 0)
    left = (n16 < 3).astype(bf16)
    right = ((n16 >= 3) & (n16 < 6)).astype(bf16)
    zero = jnp.zeros((DIM, BLK), bf16)

    @pl.loop(0, (table[0, LANES - 1] + BODY - 1) // BODY)
    def _(turn):
        for k in range(BODY):
            word = table[0, BODY * turn + k]
            p = word & (BLK - 1)
            safe = jnp.minimum(p, NBLK - 1)
            ids = [(word >> 7) & (BLK - 1), word >> 14]
            w = weights(safe)
            l16, r16 = left, right
            if pot_rows is not None:
                extra = pot_rows[safe]
                l16, r16 = left + extra, right + extra
            top = jnp.concatenate([w, zero], axis=1)
            mid = jnp.concatenate([zero, w], axis=1)
            low = jnp.concatenate([l16, r16], axis=1)
            rhs = jnp.concatenate([top, mid] + [low] * 8, axis=0)
            body = jnp.concatenate([lhs[jnp.minimum(q, NBLK - 1)] for q in ids], axis=0)
            tail = jnp.concatenate([aug[q] for q in ids], axis=0)
            both = jnp.concatenate([body, tail], axis=1)
            process(p, jnp.dot(both, rhs, preferred_element_type=f32))


def max_process(peak, total, piece):
    def process(p, v):
        old, sums = peak[p], total[p]
        for k in range(0, CHUNK * HALF, piece):
            u = v[k : k + piece].reshape(piece // 8, 8, 2 * BLK)
            top = jnp.max(u, axis=0)
            new = jnp.maximum(old, jnp.maximum(top[:, :BLK], top[:, BLK:]))
            new2 = jnp.concatenate([new, new], axis=1)
            e = jnp.sum(jnp.exp2((u - new2[None]) * C2), axis=0)
            sums = sums * jnp.exp2((old - new) * C2) + (e[:, :BLK] + e[:, BLK:])
            old = new
        peak[p] = old
        total[p] = sums

    return process


def sum_process(total):
    def process(p, v):
        u = v.reshape(CHUNK * HALF // 8, 8, 2 * BLK)
        e = jnp.sum(jnp.exp2(u * C2), axis=0)
        total[p] = total[p] + (e[:, :BLK] + e[:, BLK:])

    return process


def init_peaks(peak, total):
    peak[...] = jnp.full(peak.shape, LOW, f32)
    total[...] = jnp.zeros(total.shape, f32)


def finish_peaks(peak, total):
    m = peak[0:NBLK]
    top = jnp.max(m, axis=1)
    s = jnp.sum(total[0:NBLK] * jnp.exp2((m - top[:, None, :]) * C2), axis=1)
    return top + jnp.log2(s) * (1.0 / C2)


def finish_total(total):
    return jnp.sum(total[0:NBLK], axis=1)


def x_weights(xt):
    return lambda p: xt[:, pl.ds(pl.multiple_of(p * BLK, BLK), BLK)]


def fetch(far, table, sem):
    copy = pltpu.make_async_copy(far, table, sem.at[0])
    copy.start()
    return copy


def row1_kernel(far, b, yfold, xt, peak, total, aug, table, sem):
    listed = fetch(far, table, sem)
    fold_potential(b, aug)
    init_peaks(peak, total)
    listed.wait()
    sweep(table, yfold, aug, x_weights(xt), None, max_process(peak, total, 64))


def col1_kernel(far, a, xfold, yt, peak, total, aug, table, sem):
    listed = fetch(far, table, sem)
    fold_potential(a, aug)
    init_peaks(peak, total)
    listed.wait()
    sweep(table, xfold, aug, lambda t: yt[t], None, max_process(peak, total, 32))


def row2_kernel(far, rows, b, yfold, xt, total, aug, table, sem):
    listed = fetch(far, table, sem)
    fold_potential(b, aug)
    total[...] = jnp.zeros(total.shape, f32)
    listed.wait()
    sweep(table, yfold, aug, x_weights(xt), rows, sum_process(total))


def col2_kernel(far, rows, a, xfold, yt, xsq, total, f_out, aug, table, sem, f, f_sem):
    listed = fetch(far, table, sem)
    f[...] = a[...] * (1.0 / 32) + xsq[...] * (1.0 / 64)
    leave = pltpu.make_async_copy(f, f_out, f_sem.at[0])
    leave.start()
    fold_potential(a, aug)
    total[...] = jnp.zeros(total.shape, f32)
    listed.wait()
    sweep(table, xfold, aug, lambda t: yt[t], rows, sum_process(total))
    leave.wait()


AUG = pltpu.VMEM((NBLK + 1, HALF, BLK), bf16)
ROWS = jax.ShapeDtypeStruct((NBLK, 16, BLK), bf16)
ACC = jax.ShapeDtypeStruct((NBLK + 1, 8, BLK), f32)
TABLE = jax.ShapeDtypeStruct((1, LANES), jnp.int32)


def work_call(kernel, outs, *args, out_specs=None, scratch=()):
    return pl.pallas_call(
        kernel,
        out_shape=outs,
        in_specs=[VMEM] * len(args),
        out_specs=out_specs or jax.tree.map(lambda _: VMEM, outs),
        scratch_shapes=[AUG, pltpu.SMEM(TABLE.shape, TABLE.dtype), pltpu.SemaphoreType.DMA((1,)), *scratch],
        compiler_params=params(),
    )(*args)


def duals(n=NBLK):
    return jax.ShapeDtypeStruct((n, BLK), f32)


def place():
    i = lax.axis_index("src")
    core, z, y = lax.rem(i, 2), lax.rem(i // 2, NZ), i // (2 * NZ)
    return y, z, core


def at(y, z, core):
    return {"src": (y * NZ + z) * 2 + core}


def hail(devices):
    barrier = pltpu.get_barrier_semaphore()
    for d in devices:
        pl.semaphore_signal(barrier, inc=1, device_id=d, device_id_type=MESH)


def meet(devices):
    pl.semaphore_wait(pltpu.get_barrier_semaphore(), len(devices))


def send(src, dst, sends, recvs, k, device):
    copy = pltpu.make_async_remote_copy(
        src_ref=src, dst_ref=dst, send_sem=sends.at[k], recv_sem=recvs.at[k],
        device_id=device, device_id_type=MESH,
    )
    copy.start()
    return copy


def slot_of(dz):
    return 2 * dz - 1 if 0 < dz <= 4 else 2 * (NZ - dz) if dz else 0


GROUPS = ((0, 1), (1, 2), (3, 2), (5, 2), (7, 1))


def gather_kernel(
    own, bt_far, xt_far, yt, yfold, b0, row_table, member_ref, xt,
    held, bt_ref, ls, zs, zr, ys, yr, cs, cr,
):
    y, z, core = place()
    pick = picker()
    z_devices = {k: at(y, lax.rem(z + k, NZ), core) for k in (4, 3, 5, 2, 6, 1, 7)}
    y_devices = {k: at(lax.rem(y + k, NY), z, core) for k in (2, 1, 3)}
    mate = at(y, z, 1 - core)
    everyone = list(z_devices.values()) + list(y_devices.values()) + [mate]
    mine = held.at[0, 0, 0]
    hail(everyone)
    here = [
        pltpu.make_async_copy(src, dst, ls.at[k])
        for k, (src, dst) in enumerate(((own, mine), (bt_far, bt_ref), (xt_far, xt)))
    ]
    for c in here:
        c.start()
    here[0].wait()
    meet(everyone)

    z_copies = {}
    for k, d in z_devices.items():
        z_copies[k] = send(mine, held.at[0, 0, slot_of(NZ - k)], zs, zr, k - 1, d)
    y_copies = {}

    def on_y(g):
        first, size = GROUPS[g]
        for k, d in y_devices.items():
            part = held.at[0, 0, pl.ds(first, size)]
            dst = held.at[0, NY - k, pl.ds(first, size)]
            y_copies[k, g] = send(part, dst, ys, yr, len(GROUPS) * (k - 1) + g, d)

    c_copies = []

    def on_mate(dy, dys, first, size):
        part = held.at[0, pl.ds(dy, dys), pl.ds(first, size)]
        dst = held.at[1, pl.ds(dy, dys), pl.ds(first, size)]
        c_copies.append(send(part, dst, cs, cr, len(c_copies), mate))

    def take(side, dy, s):
        dz = (s + 1) // 2 if s % 2 else NZ - s // 2
        who = core if side == 0 else 1 - core
        t = (lax.rem(y + dy, NY) * NZ + lax.rem(z + dz, NZ)) * 2 + who
        tile = held[side, dy, s]
        yt[t] = tile
        yfold[t] = fold(pick, tile)
        wide = tile.astype(f32)
        b0[pl.ds(t, 1), :] = -0.5 * jnp.sum(wide * wide, axis=0, keepdims=True)

    def take_column(side):
        for s in range(NZ):
            take(side, 0, s)

    def take_group(side, g):
        for s in range(GROUPS[g][0], GROUPS[g][0] + GROUPS[g][1]):
            for dy in range(1, NY):
                take(side, dy, s)

    on_y(0)
    def pass_on(g):
        for k in (1, 3, 2):
            y_copies[k, g].wait_recv()
        on_mate(1, NY - 1, *GROUPS[g])

    for g, ks in ((1, (1, 7)), (2, (2, 6)), (3, (3, 5)), (4, (4,))):
        for k in ks:
            z_copies[k].wait_recv()
        on_y(g)
        if g == 2:
            pass_on(0)
    on_mate(0, 1, 0, NZ)
    here[1].wait()
    t = iota((NBLK, NBLK), 0)
    bt = bt_ref[...]
    member = sum((bt[k : k + 1, :] == t).astype(f32) for k in range(SLOTS))
    eye = (iota((NBLK, NBLK), 1) == t).astype(bf16)
    member_ref[...] = member
    row_table[...] = chunk_table(turn_over(eye, member.astype(bf16)))
    take_column(0)
    take_group(0, 0)
    pass_on(1)
    take_group(0, 1)
    c_copies[0].wait_recv()
    take_group(1, 0)
    pass_on(2)
    take_group(0, 2)
    c_copies[1].wait_recv()
    take_column(1)
    pass_on(3)
    take_group(0, 3)
    c_copies[2].wait_recv()
    take_group(1, 1)
    pass_on(4)
    take_group(0, 4)
    for g in range(2, 5):
        c_copies[1 + g].wait_recv()
        take_group(1, g)
    here[2].wait()
    for c in list(z_copies.values()) + list(y_copies.values()) + c_copies:
        c.wait_send()


def gather(own, bt, xt):
    dma = pltpu.SemaphoreType.DMA
    blocks = jax.ShapeDtypeStruct((NBLK, DIM, BLK), bf16)
    return pl.pallas_call(
        gather_kernel,
        out_shape=(blocks, blocks, duals(), TABLE, jax.ShapeDtypeStruct((NBLK, NBLK), f32), jax.ShapeDtypeStruct(xt.shape, bf16)),
        in_specs=[pl.BlockSpec(memory_space=pl.ANY)] * 3,
        out_specs=(VMEM,) * 6,
        scratch_shapes=[pltpu.VMEM((2, NY, NZ, DIM, BLK), bf16), pltpu.VMEM(bt.shape, jnp.int32)]
        + [dma((3,)), dma((7,)), dma((7,)), dma((15,)), dma((15,)), dma((6,)), dma((6,))],
        compiler_params=params(0, 50),
    )(own, bt, xt)


def spread(pairs, device_of, sends, recvs):
    for k, (src, dst) in enumerate(pairs):
        pltpu.make_async_remote_copy(
            src_ref=src, dst_ref=dst, send_sem=sends.at[0], recv_sem=recvs.at[0],
            device_id=device_of[k], device_id_type=MESH,
        ).start()


def collect(many, device, sends, recvs):
    pltpu.make_async_remote_copy(
        src_ref=many, dst_ref=many, send_sem=sends.at[0], recv_sem=recvs.at[0],
        device_id=device, device_id_type=MESH,
    ).wait()


def tgt_exchange(finish, meanwhile, mine, got, sends, recvs):
    me = lax.axis_index("tgt")
    devices = [{"tgt": lax.rem(me + k, NX)} for k in (2, 1, 3)]
    hail(devices)
    mine[...] = finish().astype(mine.dtype)
    meet(devices)
    spread([(mine, got.at[me])] * 3, devices, sends, recvs)
    got[me] = mine[...]
    meanwhile()
    collect(got.at[pl.ds(0, 3)], devices[0], sends, recvs)


def tgt1_kernel(peak, total, xt, member, a_ref, xfold, xsq, col_table, mine, got, sends, recvs):
    pick = picker()

    def meanwhile():
        col_table[...] = chunk_table(member[...])

        @pl.loop(0, NBLK, step=8)
        def _(p):
            for i in range(8):
                tile = xt[:, pl.ds(pl.multiple_of((p + i) * BLK, BLK), BLK)]
                xfold[p + i] = fold(pick, tile)
                wide = tile.astype(f32)
                xsq[pl.ds(p + i, 1), :] = jnp.sum(wide * wide, axis=0, keepdims=True)

    tgt_exchange(lambda: finish_peaks(peak, total), meanwhile, mine, got, sends, recvs)
    a_ref[...] = -lse([got[k] for k in range(NX)]) - LOG_NS


def tgt2_kernel(total, old, b_ref, a_ref, rows, mine, got, sends, recvs):
    tgt_exchange(
        lambda: finish_total(total), lambda: spread_rows(b_ref, rows), mine, got, sends, recvs
    )
    g0, g1, g2, g3 = (got[k].astype(f32) for k in range(NX))
    s = (g0 + g1) + (g2 + g3)
    a_ref[...] = old[...] - jnp.log2(s * NS) * (1.0 / C2)


def tgt_call(kernel, collective_id, kind, outs, *args):
    dma = pltpu.SemaphoreType.DMA
    mine = pltpu.VMEM((NBLK, BLK), kind)
    return pl.pallas_call(
        kernel,
        out_shape=outs,
        in_specs=[VMEM] * len(args),
        out_specs=jax.tree.map(lambda _: VMEM, outs),
        scratch_shapes=[mine, pltpu.VMEM((NX, NBLK, BLK), kind), dma((1,)), dma((1,))],
        compiler_params=params(collective_id),
    )(*args)


def lse(parts):
    top = functools.reduce(jnp.maximum, parts)
    s = sum(jnp.exp2((v - top) * C2) for v in parts)
    return top + jnp.log2(s) * (1.0 / C2)


def mates():
    y, z, core = place()
    m = y * 2 + core

    def side(k):
        other = lax.rem(m + k, 8)
        return other, at(other // 2, z, lax.rem(other, 2))

    def up(k):
        other = lax.rem(z + k, NZ)
        return other, at(y, other, core)

    far_first = (4, 3, 5, 2, 6, 1, 7)
    return m, z, [side(k) for k in far_first], [up(k) for k in far_first]


def rows_of(k):
    return pl.ds((k // 2) * 2 * NZ + k % 2, NZ, stride=2)


def scatter_sides(finish, combine, m, sides, ups, mine, order, r1, sends, recvs):
    devices = [d for _, d in ups + sides]
    hail(devices)
    mine[...] = finish()
    for k in range(8):
        order[k] = mine[rows_of(k), :]
    meet(devices)
    spread([(order.at[o], r1.at[m]) for o, _ in sides], [d for _, d in sides], sends, recvs)
    r1[m] = order[m]
    collect(r1.at[pl.ds(0, 7)], sides[0][1], sends, recvs)
    return combine([r1[k] for k in range(8)])


def src1_kernel(peak, total, a_ref, b_ref, own_ref, a_rows, mine, order, r1, tile, r2, done, r4, s1, q1, s2, q2, s3, q3):
    m, z, sides, ups = mates()
    tile[...] = scatter_sides(
        lambda: finish_peaks(peak, total), lse, m, sides, ups, mine, order, r1, s1, q1
    )
    spread([(tile, r2.at[z])] * 7, [d for _, d in ups], s2, q2)
    r2[z] = tile[...]
    spread_rows(a_ref, a_rows)
    collect(r2.at[pl.ds(0, 7)], ups[0][1], s2, q2)
    done[...] = -lse([r2[k] for k in range(8)]) - LOG_NT
    spread([(done, r4.at[m])] * 7, [d for _, d in sides], s3, q3)
    r4[m] = done[...]
    own_ref[...] = jnp.broadcast_to(done[pl.ds(z, 1), :], (8, BLK))
    collect(r4.at[pl.ds(0, 7)], sides[0][1], s3, q3)
    for k in range(8):
        b_ref[rows_of(k), :] = r4[k]


def src2_kernel(total, old, yt_ref, g_ref, mine, order, r1, rows, r2, s1, q1, s2, q2):
    m, z, sides, ups = mates()
    first = scatter_sides(
        lambda: finish_total(total), sum, m, sides, ups, mine, order, r1, s1, q1
    )
    for k in range(8):
        rows[k] = jnp.broadcast_to(first[k : k + 1], (8, BLK))
    spread([(rows.at[o], r2.at[z]) for o, _ in ups], [d for _, d in ups], s2, q2)
    r2[z] = rows[z]
    y = yt_ref[...].astype(f32)
    sq = jnp.sum(y * y, axis=0, keepdims=True)
    collect(r2.at[pl.ds(0, 7)], ups[0][1], s2, q2)
    s = sum([r2[k] for k in range(8)])
    b = old[...] - jnp.log2(s * NT) * (1.0 / C2)
    g_ref[...] = b * (1.0 / 32) + sq * (1.0 / 64)


def src_call(kernel, collective_id, outs, scratch, phases, *args):
    mine = pltpu.VMEM((NBLK, BLK), f32)
    return pl.pallas_call(
        kernel,
        out_shape=outs,
        in_specs=[VMEM] * len(args),
        out_specs=jax.tree.map(lambda _: VMEM, outs),
        scratch_shapes=[mine] + scratch + [pltpu.SemaphoreType.DMA((1,))] * (2 * phases),
        compiler_params=params(collective_id),
    )(*args)


def local(source_features, target_features, block_targets):
    own_yt = target_features[0].T
    block, tile = pltpu.VMEM((8, 8, BLK), f32), pltpu.VMEM((8, BLK), f32)

    blocks = jax.ShapeDtypeStruct((NBLK, DIM, BLK), bf16)
    yt, yfold, b0, row_table, member, xt = gather(
        own_yt, block_targets[:, 0, :].T, source_features.T
    )
    peak, total = work_call(row1_kernel, (ACC, ACC), row_table, b0, yfold, xt)
    a, xfold, xsq, col_table = tgt_call(
        tgt1_kernel, 1, f32, (duals(), blocks, duals(), TABLE), peak, total, xt, member
    )
    peak, total = work_call(col1_kernel, (ACC, ACC), col_table, a, xfold, yt)
    b, own, rows = src_call(
        src1_kernel, 2, (duals(), duals(8), ROWS), [block, block, tile, block, tile, block], 3,
        peak, total, a,
    )
    total = work_call(row2_kernel, ACC, row_table, rows, b, yfold, xt)
    a, rows = tgt_call(tgt2_kernel, 3, bf16, (duals(), ROWS), total, a, b)
    total, f = work_call(
        col2_kernel, (ACC, duals()), col_table, rows, a, xfold, yt, xsq,
        out_specs=(VMEM, pl.BlockSpec(memory_space=pl.ANY)),
        scratch=(pltpu.VMEM((NBLK, BLK), f32), pltpu.SemaphoreType.DMA((1,))),
    )
    g = src_call(src2_kernel, 4, duals(8), [block] * 4, 2, total, own, own_yt)
    return f.reshape(-1), g[0:1]


def solution(mesh):
    in_specs = (P("src", None), P("tgt", "src", None), P("src", "tgt", None))
    out_specs = (P("src"), P("tgt", "src"))
    return jax.shard_map(local, mesh=mesh, in_specs=in_specs, out_specs=out_specs, check_vma=False)
```

```python
import functools
import math

import jax
import jax.numpy as jnp
from jax import lax
from jax.experimental import pallas as pl
from jax.experimental.pallas import tpu as pltpu
from jax.sharding import PartitionSpec as P

BLK = 128
DIM = 64
HALF = BLK // 2
NBLK = 64
SLOTS = 8
CHUNK = 2
LANES = 384
EPSILON = 0.01
NS = 524288
NT = 32768
NY, NZ, NX = 4, 8, 4
RATE = 2.0 / (DIM * EPSILON)
C2 = RATE / math.log(2.0)
LOG_NS = math.log(NS) / RATE
LOG_NT = math.log(NT) / RATE
LOW = -1.0e30
BODY = 96
REST = 16
MESH = pl.DeviceIdType.MESH
VMEM = pl.BlockSpec(memory_space=pltpu.VMEM)
f32, bf16 = jnp.float32, jnp.bfloat16


def iota(shape, dim):
    return lax.broadcasted_iota(jnp.int32, shape, dim)


def pieces(v):
    hi = v.astype(bf16).astype(f32)
    rest = v - hi
    mid = rest.astype(bf16).astype(f32)
    return hi, mid, rest - mid


def params(collective_id=None, limit=40):
    if collective_id is None:
        return pltpu.CompilerParams(vmem_limit_bytes=limit << 20)
    return pltpu.CompilerParams(
        vmem_limit_bytes=limit << 20, collective_id=collective_id, has_side_effects=True
    )


def picker():
    return (iota((HALF, BLK), 1) % HALF == iota((HALF, BLK), 0)).astype(bf16)


def turn_over(pick, rows):
    return lax.dot_general(pick, rows, (((1,), (1,)), ((), ())), preferred_element_type=f32)


def fold(pick, tile):
    low = (iota((DIM, BLK), 1) < HALF).astype(bf16)
    rows = jnp.concatenate([tile * low, tile * (1.0 - low).astype(bf16)], axis=0)
    return turn_over(pick, rows).astype(bf16)


def fold_potential(pot, aug):
    lane = iota((HALF, BLK), 1)
    pick = picker()
    n = iota((8, 16, BLK), 1)
    h = iota((8, 16, BLK), 2) // HALF
    keep = ((n < 6) & (n // 3 == h)) | ((n >= 6) & (n < 9) & (h == 0))
    for g in range(8):
        hi, mid, lo = (v[:, None, :] for v in pieces(pot[8 * g : 8 * g + 8, :]))
        rows = jnp.where(
            n >= 6, 1.0, jnp.where(n % 3 == 0, hi, jnp.where(n % 3 == 1, mid, lo))
        )
        rows = jnp.where(keep, rows, 0.0).reshape(BLK, BLK).astype(bf16)
        turned = turn_over(pick, rows)
        for k in range(8):
            aug[8 * g + k] = jnp.where(lane // 16 == k, turned, 0.0).astype(bf16)
    n = iota((HALF, BLK), 1)
    aug[NBLK] = jnp.where((n == 0) | (n == 3), LOW, 0.0).astype(bf16)


def spread_rows(pot, rows):
    n = iota((8, 16, BLK), 1)
    for g in range(8):
        hi, mid, lo = (v[:, None, :] for v in pieces(pot[8 * g : 8 * g + 8, :]))
        v = jnp.where(n == 6, hi, jnp.where(n == 7, mid, jnp.where(n == 8, lo, 0.0)))
        rows[8 * g : 8 * g + 8] = v.astype(bf16)


def chunk_table(member):
    dot = functools.partial(jnp.dot, preferred_element_type=f32)
    m = member.astype(bf16)
    up = (iota((NBLK, NBLK), 0) < iota((NBLK, NBLK), 1)).astype(bf16)
    upto = (iota((NBLK, NBLK), 0) >= iota((NBLK, NBLK), 1)).astype(bf16)
    eye = (iota((NBLK, NBLK), 0) == iota((NBLK, NBLK), 1)).astype(bf16)
    place_of = (member * (dot(m, up) + 1.0)).astype(bf16)
    turned = turn_over(eye, place_of).astype(bf16)
    size = dot(m, jnp.ones((NBLK, LANES), bf16))
    many = jnp.floor((size + (CHUNK - 1.0)) * (1.0 / CHUNK))
    end = dot(upto, many.astype(bf16))
    row = iota((NBLK, LANES), 0).astype(f32)
    n = iota((NBLK, LANES), 1).astype(f32)
    before = (end <= n).astype(f32)
    p = jnp.sum(before, axis=0, keepdims=True)
    first = CHUNK * (n[:1] - jnp.sum(before * many, axis=0, keepdims=True))
    mine = dot(turned, (row == p).astype(bf16))
    rows = [
        NBLK + jnp.sum((row - NBLK) * (mine == first + (k + 1.0)).astype(f32), axis=0, keepdims=True)
        for k in range(CHUNK)
    ]
    word = p + BLK * (rows[0] + BLK * rows[1])
    return jnp.where(n[:1] == LANES - 1, end[NBLK - 1 :], word).astype(jnp.int32)


def sweep(table, lhs, aug, weights, pot_rows, process):
    n16 = iota((16, BLK), 0)
    left = (n16 < 3).astype(bf16)
    right = ((n16 >= 3) & (n16 < 6)).astype(bf16)
    zero = jnp.zeros((DIM, BLK), bf16)

    def work(n):
        word = table[0, n]
        p = word & (BLK - 1)
        safe = jnp.minimum(p, NBLK - 1)
        ids = [(word >> 7) & (BLK - 1), word >> 14]
        w = weights(safe)
        l16, r16 = left, right
        if pot_rows is not None:
            extra = pot_rows[safe]
            l16, r16 = left + extra, right + extra
        top = jnp.concatenate([w, zero], axis=1)
        mid = jnp.concatenate([zero, w], axis=1)
        low = jnp.concatenate([l16, r16], axis=1)
        rhs = jnp.concatenate([top, mid] + [low] * 8, axis=0)
        body = jnp.concatenate([lhs[jnp.minimum(q, NBLK - 1)] for q in ids], axis=0)
        tail = jnp.concatenate([aug[q] for q in ids], axis=0)
        both = jnp.concatenate([body, tail], axis=1)
        process(p, jnp.dot(both, rhs, preferred_element_type=f32))

    count = table[0, LANES - 1]
    full = (count + BODY - 1 - 2 * REST) // BODY
    done = BODY * full

    @pl.loop(0, full)
    def _(turn):
        for k in range(BODY):
            work(BODY * turn + k)

    @pl.loop(0, jnp.maximum(count - done + REST - 1, 0) // REST)
    def _(turn):
        for k in range(REST):
            work(done + REST * turn + k)


def max_process(peak, total, piece):
    def process(p, v):
        old, sums = peak[p], total[p]
        for k in range(0, CHUNK * HALF, piece):
            u = v[k : k + piece].reshape(piece // 8, 8, 2 * BLK)
            top = jnp.max(u, axis=0)
            new = jnp.maximum(old, jnp.maximum(top[:, :BLK], top[:, BLK:]))
            new2 = jnp.concatenate([new, new], axis=1)
            e = jnp.sum(jnp.exp2((u - new2[None]) * C2), axis=0)
            sums = sums * jnp.exp2((old - new) * C2) + (e[:, :BLK] + e[:, BLK:])
            old = new
        peak[p] = old
        total[p] = sums

    return process


def sum_process(total):
    def process(p, v):
        u = v.reshape(CHUNK * HALF // 8, 8, 2 * BLK)
        e = jnp.sum(jnp.exp2(u * C2), axis=0)
        total[p] = total[p] + (e[:, :BLK] + e[:, BLK:])

    return process


def init_peaks(peak, total):
    peak[...] = jnp.full(peak.shape, LOW, f32)
    total[...] = jnp.zeros(total.shape, f32)


def finish_peaks(peak, total):
    m = peak[0:NBLK]
    top = jnp.max(m, axis=1)
    s = jnp.sum(total[0:NBLK] * jnp.exp2((m - top[:, None, :]) * C2), axis=1)
    return top + jnp.log2(s) * (1.0 / C2)


def finish_total(total):
    return jnp.sum(total[0:NBLK], axis=1)


def x_weights(xt):
    return lambda p: xt[:, pl.ds(pl.multiple_of(p * BLK, BLK), BLK)]


def fetch(far, table, sem):
    copy = pltpu.make_async_copy(far, table, sem.at[0])
    copy.start()
    return copy


def row1_kernel(far, b, yfold, xt, peak, total, aug, table, sem):
    listed = fetch(far, table, sem)
    fold_potential(b, aug)
    init_peaks(peak, total)
    listed.wait()
    sweep(table, yfold, aug, x_weights(xt), None, max_process(peak, total, 64))


def col1_kernel(far, a, xfold, yt, peak, total, aug, table, sem):
    listed = fetch(far, table, sem)
    fold_potential(a, aug)
    init_peaks(peak, total)
    listed.wait()
    sweep(table, xfold, aug, lambda t: yt[t], None, max_process(peak, total, 32))


def row2_kernel(far, rows, b, yfold, xt, total, aug, table, sem):
    listed = fetch(far, table, sem)
    fold_potential(b, aug)
    total[...] = jnp.zeros(total.shape, f32)
    listed.wait()
    sweep(table, yfold, aug, x_weights(xt), rows, sum_process(total))


def col2_kernel(far, rows, a, xfold, yt, xsq, total, f_out, aug, table, sem, f, f_sem):
    listed = fetch(far, table, sem)
    f[...] = a[...] * (1.0 / 32) + xsq[...] * (1.0 / 64)
    leave = pltpu.make_async_copy(f, f_out, f_sem.at[0])
    leave.start()
    fold_potential(a, aug)
    total[...] = jnp.zeros(total.shape, f32)
    listed.wait()
    sweep(table, xfold, aug, lambda t: yt[t], rows, sum_process(total))
    leave.wait()


AUG = pltpu.VMEM((NBLK + 1, HALF, BLK), bf16)
ROWS = jax.ShapeDtypeStruct((NBLK, 16, BLK), bf16)
ACC = jax.ShapeDtypeStruct((NBLK + 1, 8, BLK), f32)
TABLE = jax.ShapeDtypeStruct((1, LANES), jnp.int32)


def work_call(kernel, outs, *args, out_specs=None, scratch=()):
    return pl.pallas_call(
        kernel,
        out_shape=outs,
        in_specs=[VMEM] * len(args),
        out_specs=out_specs or jax.tree.map(lambda _: VMEM, outs),
        scratch_shapes=[AUG, pltpu.SMEM(TABLE.shape, TABLE.dtype), pltpu.SemaphoreType.DMA((1,)), *scratch],
        compiler_params=params(),
    )(*args)


def duals(n=NBLK):
    return jax.ShapeDtypeStruct((n, BLK), f32)


def place():
    i = lax.axis_index("src")
    core, z, y = lax.rem(i, 2), lax.rem(i // 2, NZ), i // (2 * NZ)
    return y, z, core


def at(y, z, core):
    return {"src": (y * NZ + z) * 2 + core}


def hail(devices):
    barrier = pltpu.get_barrier_semaphore()
    for d in devices:
        pl.semaphore_signal(barrier, inc=1, device_id=d, device_id_type=MESH)


def meet(devices):
    pl.semaphore_wait(pltpu.get_barrier_semaphore(), len(devices))


def send(src, dst, sends, recvs, k, device):
    copy = pltpu.make_async_remote_copy(
        src_ref=src, dst_ref=dst, send_sem=sends.at[k], recv_sem=recvs.at[k],
        device_id=device, device_id_type=MESH,
    )
    copy.start()
    return copy


def slot_of(dz):
    return 2 * dz - 1 if 0 < dz <= 4 else 2 * (NZ - dz) if dz else 0


GROUPS = ((0, 1), (1, 2), (3, 2), (5, 2), (7, 1))


def gather_kernel(
    own, bt_far, xt_far, yt, yfold, b0, row_table, member_ref, xt,
    held, bt_ref, ls, zs, zr, ys, yr, cs, cr,
):
    y, z, core = place()
    pick = picker()
    z_devices = {k: at(y, lax.rem(z + k, NZ), core) for k in (4, 3, 5, 2, 6, 1, 7)}
    y_devices = {k: at(lax.rem(y + k, NY), z, core) for k in (2, 1, 3)}
    mate = at(y, z, 1 - core)
    everyone = list(z_devices.values()) + list(y_devices.values()) + [mate]
    mine = held.at[0, 0, 0]
    hail(everyone)
    here = [
        pltpu.make_async_copy(src, dst, ls.at[k])
        for k, (src, dst) in enumerate(((own, mine), (bt_far, bt_ref), (xt_far, xt)))
    ]
    for c in here:
        c.start()
    here[0].wait()
    meet(everyone)

    z_copies = {}
    for k, d in z_devices.items():
        z_copies[k] = send(mine, held.at[0, 0, slot_of(NZ - k)], zs, zr, k - 1, d)
    y_copies = {}

    def on_y(g):
        first, size = GROUPS[g]
        for k, d in y_devices.items():
            part = held.at[0, 0, pl.ds(first, size)]
            dst = held.at[0, NY - k, pl.ds(first, size)]
            y_copies[k, g] = send(part, dst, ys, yr, len(GROUPS) * (k - 1) + g, d)

    c_copies = []

    def on_mate(dy, dys, first, size):
        part = held.at[0, pl.ds(dy, dys), pl.ds(first, size)]
        dst = held.at[1, pl.ds(dy, dys), pl.ds(first, size)]
        c_copies.append(send(part, dst, cs, cr, len(c_copies), mate))

    def take(side, dy, s):
        dz = (s + 1) // 2 if s % 2 else NZ - s // 2
        who = core if side == 0 else 1 - core
        t = (lax.rem(y + dy, NY) * NZ + lax.rem(z + dz, NZ)) * 2 + who
        tile = held[side, dy, s]
        yt[t] = tile
        yfold[t] = fold(pick, tile)
        wide = tile.astype(f32)
        b0[pl.ds(t, 1), :] = -0.5 * jnp.sum(wide * wide, axis=0, keepdims=True)

    def take_column(side):
        for s in range(NZ):
            take(side, 0, s)

    def take_group(side, g):
        for s in range(GROUPS[g][0], GROUPS[g][0] + GROUPS[g][1]):
            for dy in range(1, NY):
                take(side, dy, s)

    on_y(0)
    def pass_on(g):
        for k in (1, 3, 2):
            y_copies[k, g].wait_recv()
        on_mate(1, NY - 1, *GROUPS[g])

    for g, ks in ((1, (1, 7)), (2, (2, 6)), (3, (3, 5)), (4, (4,))):
        for k in ks:
            z_copies[k].wait_recv()
        on_y(g)
        if g == 2:
            pass_on(0)
    on_mate(0, 1, 0, NZ)
    here[1].wait()
    t = iota((NBLK, NBLK), 0)
    bt = bt_ref[...]
    member = sum((bt[k : k + 1, :] == t).astype(f32) for k in range(SLOTS))
    eye = (iota((NBLK, NBLK), 1) == t).astype(bf16)
    member_ref[...] = member
    row_table[...] = chunk_table(turn_over(eye, member.astype(bf16)))
    take_column(0)
    take_group(0, 0)
    pass_on(1)
    take_group(0, 1)
    c_copies[0].wait_recv()
    take_group(1, 0)
    pass_on(2)
    take_group(0, 2)
    c_copies[1].wait_recv()
    take_column(1)
    pass_on(3)
    take_group(0, 3)
    c_copies[2].wait_recv()
    take_group(1, 1)
    pass_on(4)
    take_group(0, 4)
    for g in range(2, 5):
        c_copies[1 + g].wait_recv()
        take_group(1, g)
    here[2].wait()
    for c in list(z_copies.values()) + list(y_copies.values()) + c_copies:
        c.wait_send()


def gather(own, bt, xt):
    dma = pltpu.SemaphoreType.DMA
    blocks = jax.ShapeDtypeStruct((NBLK, DIM, BLK), bf16)
    return pl.pallas_call(
        gather_kernel,
        out_shape=(blocks, blocks, duals(), TABLE, jax.ShapeDtypeStruct((NBLK, NBLK), f32), jax.ShapeDtypeStruct(xt.shape, bf16)),
        in_specs=[pl.BlockSpec(memory_space=pl.ANY)] * 3,
        out_specs=(VMEM,) * 6,
        scratch_shapes=[pltpu.VMEM((2, NY, NZ, DIM, BLK), bf16), pltpu.VMEM(bt.shape, jnp.int32)]
        + [dma((3,)), dma((7,)), dma((7,)), dma((15,)), dma((15,)), dma((6,)), dma((6,))],
        compiler_params=params(0, 50),
    )(own, bt, xt)


def spread(pairs, device_of, sends, recvs):
    for k, (src, dst) in enumerate(pairs):
        pltpu.make_async_remote_copy(
            src_ref=src, dst_ref=dst, send_sem=sends.at[0], recv_sem=recvs.at[0],
            device_id=device_of[k], device_id_type=MESH,
        ).start()


def collect(many, device, sends, recvs):
    pltpu.make_async_remote_copy(
        src_ref=many, dst_ref=many, send_sem=sends.at[0], recv_sem=recvs.at[0],
        device_id=device, device_id_type=MESH,
    ).wait()


def tgt_exchange(finish, meanwhile, mine, got, sends, recvs):
    me = lax.axis_index("tgt")
    devices = [{"tgt": lax.rem(me + k, NX)} for k in (2, 1, 3)]
    hail(devices)
    mine[...] = finish().astype(mine.dtype)
    meet(devices)
    spread([(mine, got.at[me])] * 3, devices, sends, recvs)
    got[me] = mine[...]
    meanwhile()
    collect(got.at[pl.ds(0, 3)], devices[0], sends, recvs)


def tgt1_kernel(peak, total, xt, member, a_ref, xfold, xsq, col_table, mine, got, sends, recvs):
    pick = picker()

    def meanwhile():
        col_table[...] = chunk_table(member[...])

        @pl.loop(0, NBLK, step=8)
        def _(p):
            for i in range(8):
                tile = xt[:, pl.ds(pl.multiple_of((p + i) * BLK, BLK), BLK)]
                xfold[p + i] = fold(pick, tile)
                wide = tile.astype(f32)
                xsq[pl.ds(p + i, 1), :] = jnp.sum(wide * wide, axis=0, keepdims=True)

    tgt_exchange(lambda: finish_peaks(peak, total), meanwhile, mine, got, sends, recvs)
    a_ref[...] = -lse([got[k] for k in range(NX)]) - LOG_NS


def tgt2_kernel(total, old, b_ref, a_ref, rows, mine, got, sends, recvs):
    tgt_exchange(
        lambda: finish_total(total), lambda: spread_rows(b_ref, rows), mine, got, sends, recvs
    )
    g0, g1, g2, g3 = (got[k].astype(f32) for k in range(NX))
    s = (g0 + g1) + (g2 + g3)
    a_ref[...] = old[...] - jnp.log2(s * NS) * (1.0 / C2)


def tgt_call(kernel, collective_id, kind, outs, *args):
    dma = pltpu.SemaphoreType.DMA
    mine = pltpu.VMEM((NBLK, BLK), kind)
    return pl.pallas_call(
        kernel,
        out_shape=outs,
        in_specs=[VMEM] * len(args),
        out_specs=jax.tree.map(lambda _: VMEM, outs),
        scratch_shapes=[mine, pltpu.VMEM((NX, NBLK, BLK), kind), dma((1,)), dma((1,))],
        compiler_params=params(collective_id),
    )(*args)


def lse(parts):
    top = functools.reduce(jnp.maximum, parts)
    s = sum(jnp.exp2((v - top) * C2) for v in parts)
    return top + jnp.log2(s) * (1.0 / C2)


def mates():
    y, z, core = place()
    m = y * 2 + core

    def side(k):
        other = lax.rem(m + k, 8)
        return other, at(other // 2, z, lax.rem(other, 2))

    def up(k):
        other = lax.rem(z + k, NZ)
        return other, at(y, other, core)

    far_first = (4, 3, 5, 2, 6, 1, 7)
    return m, z, [side(k) for k in far_first], [up(k) for k in far_first]


def rows_of(k):
    return pl.ds((k // 2) * 2 * NZ + k % 2, NZ, stride=2)


def scatter_sides(finish, combine, m, sides, ups, mine, order, r1, sends, recvs):
    devices = [d for _, d in ups + sides]
    hail(devices)
    mine[...] = finish()
    for k in range(8):
        order[k] = mine[rows_of(k), :]
    meet(devices)
    spread([(order.at[o], r1.at[m]) for o, _ in sides], [d for _, d in sides], sends, recvs)
    r1[m] = order[m]
    collect(r1.at[pl.ds(0, 7)], sides[0][1], sends, recvs)
    return combine([r1[k] for k in range(8)])


def src1_kernel(peak, total, a_ref, b_ref, own_ref, a_rows, mine, order, r1, tile, r2, done, r4, s1, q1, s2, q2, s3, q3):
    m, z, sides, ups = mates()
    tile[...] = scatter_sides(
        lambda: finish_peaks(peak, total), lse, m, sides, ups, mine, order, r1, s1, q1
    )
    spread([(tile, r2.at[z])] * 7, [d for _, d in ups], s2, q2)
    r2[z] = tile[...]
    spread_rows(a_ref, a_rows)
    collect(r2.at[pl.ds(0, 7)], ups[0][1], s2, q2)
    done[...] = -lse([r2[k] for k in range(8)]) - LOG_NT
    spread([(done, r4.at[m])] * 7, [d for _, d in sides], s3, q3)
    r4[m] = done[...]
    own_ref[...] = jnp.broadcast_to(done[pl.ds(z, 1), :], (8, BLK))
    collect(r4.at[pl.ds(0, 7)], sides[0][1], s3, q3)
    for k in range(8):
        b_ref[rows_of(k), :] = r4[k]


def src2_kernel(total, old, yt_ref, g_ref, mine, order, r1, rows, r2, s1, q1, s2, q2):
    m, z, sides, ups = mates()
    first = scatter_sides(
        lambda: finish_total(total), sum, m, sides, ups, mine, order, r1, s1, q1
    )
    for k in range(8):
        rows[k] = jnp.broadcast_to(first[k : k + 1], (8, BLK))
    spread([(rows.at[o], r2.at[z]) for o, _ in ups], [d for _, d in ups], s2, q2)
    r2[z] = rows[z]
    y = yt_ref[...].astype(f32)
    sq = jnp.sum(y * y, axis=0, keepdims=True)
    collect(r2.at[pl.ds(0, 7)], ups[0][1], s2, q2)
    s = sum([r2[k] for k in range(8)])
    b = old[...] - jnp.log2(s * NT) * (1.0 / C2)
    g_ref[...] = b * (1.0 / 32) + sq * (1.0 / 64)


def src_call(kernel, collective_id, outs, scratch, phases, *args):
    mine = pltpu.VMEM((NBLK, BLK), f32)
    return pl.pallas_call(
        kernel,
        out_shape=outs,
        in_specs=[VMEM] * len(args),
        out_specs=jax.tree.map(lambda _: VMEM, outs),
        scratch_shapes=[mine] + scratch + [pltpu.SemaphoreType.DMA((1,))] * (2 * phases),
        compiler_params=params(collective_id),
    )(*args)


def local(source_features, target_features, block_targets):
    own_yt = target_features[0].T
    block, tile = pltpu.VMEM((8, 8, BLK), f32), pltpu.VMEM((8, BLK), f32)

    blocks = jax.ShapeDtypeStruct((NBLK, DIM, BLK), bf16)
    yt, yfold, b0, row_table, member, xt = gather(
        own_yt, block_targets[:, 0, :].T, source_features.T
    )
    peak, total = work_call(row1_kernel, (ACC, ACC), row_table, b0, yfold, xt)
    a, xfold, xsq, col_table = tgt_call(
        tgt1_kernel, 1, f32, (duals(), blocks, duals(), TABLE), peak, total, xt, member
    )
    peak, total = work_call(col1_kernel, (ACC, ACC), col_table, a, xfold, yt)
    b, own, rows = src_call(
        src1_kernel, 2, (duals(), duals(8), ROWS), [block, block, tile, block, tile, block], 3,
        peak, total, a,
    )
    total = work_call(row2_kernel, ACC, row_table, rows, b, yfold, xt)
    a, rows = tgt_call(tgt2_kernel, 3, bf16, (duals(), ROWS), total, a, b)
    total, f = work_call(
        col2_kernel, (ACC, duals()), col_table, rows, a, xfold, yt, xsq,
        out_specs=(VMEM, pl.BlockSpec(memory_space=pl.ANY)),
        scratch=(pltpu.VMEM((NBLK, BLK), f32), pltpu.SemaphoreType.DMA((1,))),
    )
    g = src_call(src2_kernel, 4, duals(8), [block] * 4, 2, total, own, own_yt)
    return f.reshape(-1), g[0:1]


def solution(mesh):
    in_specs = (P("src", None), P("tgt", "src", None), P("src", "tgt", None))
    out_specs = (P("src"), P("tgt", "src"))
    return jax.shard_map(local, mesh=mesh, in_specs=in_specs, out_specs=out_specs, check_vma=False)
```

```python
import functools
import math

import jax
import jax.numpy as jnp
from jax import lax
from jax.experimental import pallas as pl
from jax.experimental.pallas import tpu as pltpu
from jax.sharding import PartitionSpec as P

BLK = 128
DIM = 64
HALF = BLK // 2
NBLK = 64
SLOTS = 8
CHUNK = 2
LANES = 384
EPSILON = 0.01
NS = 524288
NT = 32768
NY, NZ, NX = 4, 8, 4
RATE = 2.0 / (DIM * EPSILON)
C2 = RATE / math.log(2.0)
LOG_NS = math.log(NS) / RATE
LOG_NT = math.log(NT) / RATE
LOW = -1.0e30
BODY = 96
REST = 16
MESH = pl.DeviceIdType.MESH
VMEM = pl.BlockSpec(memory_space=pltpu.VMEM)
f32, bf16 = jnp.float32, jnp.bfloat16


def iota(shape, dim):
    return lax.broadcasted_iota(jnp.int32, shape, dim)


def pieces(v):
    hi = v.astype(bf16).astype(f32)
    rest = v - hi
    mid = rest.astype(bf16).astype(f32)
    return hi, mid, rest - mid


def params(collective_id=None, limit=40):
    if collective_id is None:
        return pltpu.CompilerParams(vmem_limit_bytes=limit << 20)
    return pltpu.CompilerParams(
        vmem_limit_bytes=limit << 20, collective_id=collective_id, has_side_effects=True
    )


def picker():
    return (iota((HALF, BLK), 1) % HALF == iota((HALF, BLK), 0)).astype(bf16)


def turn_over(pick, rows):
    return lax.dot_general(pick, rows, (((1,), (1,)), ((), ())), preferred_element_type=f32)


def fold(pick, tile):
    low = (iota((DIM, BLK), 1) < HALF).astype(bf16)
    rows = jnp.concatenate([tile * low, tile * (1.0 - low).astype(bf16)], axis=0)
    return turn_over(pick, rows).astype(bf16)


def fold_potential(pot, aug):
    lane = iota((HALF, BLK), 1)
    pick = picker()
    n = iota((8, 16, BLK), 1)
    h = iota((8, 16, BLK), 2) // HALF
    keep = ((n < 6) & (n // 3 == h)) | ((n >= 6) & (n < 9) & (h == 0))
    for g in range(8):
        hi, mid, lo = (v[:, None, :] for v in pieces(pot[8 * g : 8 * g + 8, :]))
        rows = jnp.where(
            n >= 6, 1.0, jnp.where(n % 3 == 0, hi, jnp.where(n % 3 == 1, mid, lo))
        )
        rows = jnp.where(keep, rows, 0.0).reshape(BLK, BLK).astype(bf16)
        turned = turn_over(pick, rows)
        for k in range(8):
            aug[8 * g + k] = jnp.where(lane // 16 == k, turned, 0.0).astype(bf16)
    n = iota((HALF, BLK), 1)
    aug[NBLK] = jnp.where((n == 0) | (n == 3), LOW, 0.0).astype(bf16)


def spread_rows(pot, rows):
    n = iota((8, 16, BLK), 1)
    for g in range(8):
        hi, mid, lo = (v[:, None, :] for v in pieces(pot[8 * g : 8 * g + 8, :]))
        v = jnp.where(n == 6, hi, jnp.where(n == 7, mid, jnp.where(n == 8, lo, 0.0)))
        rows[8 * g : 8 * g + 8] = v.astype(bf16)


def chunk_table(member):
    dot = functools.partial(jnp.dot, preferred_element_type=f32)
    m = member.astype(bf16)
    up = (iota((NBLK, NBLK), 0) < iota((NBLK, NBLK), 1)).astype(bf16)
    upto = (iota((NBLK, NBLK), 0) >= iota((NBLK, NBLK), 1)).astype(bf16)
    eye = (iota((NBLK, NBLK), 0) == iota((NBLK, NBLK), 1)).astype(bf16)
    place_of = (member * (dot(m, up) + 1.0)).astype(bf16)
    turned = turn_over(eye, place_of).astype(bf16)
    size = dot(m, jnp.ones((NBLK, LANES), bf16))
    many = jnp.floor((size + (CHUNK - 1.0)) * (1.0 / CHUNK))
    end = dot(upto, many.astype(bf16))
    row = iota((NBLK, LANES), 0).astype(f32)
    n = iota((NBLK, LANES), 1).astype(f32)
    before = (end <= n).astype(f32)
    p = jnp.sum(before, axis=0, keepdims=True)
    first = CHUNK * (n[:1] - jnp.sum(before * many, axis=0, keepdims=True))
    mine = dot(turned, (row == p).astype(bf16))
    rows = [
        NBLK + jnp.sum((row - NBLK) * (mine == first + (k + 1.0)).astype(f32), axis=0, keepdims=True)
        for k in range(CHUNK)
    ]
    word = p + BLK * (rows[0] + BLK * rows[1])
    return jnp.where(n[:1] == LANES - 1, end[NBLK - 1 :], word).astype(jnp.int32)


def sweep(table, lhs, aug, weights, pot_rows, process):
    n16 = iota((16, BLK), 0)
    left = (n16 < 3).astype(bf16)
    right = ((n16 >= 3) & (n16 < 6)).astype(bf16)
    zero = jnp.zeros((DIM, BLK), bf16)

    def work(n, bank):
        word = table[0, n]
        p = word & (BLK - 1)
        safe = jnp.minimum(p, NBLK - 1)
        ids = [(word >> 7) & (BLK - 1), word >> 14]
        w = weights(safe)
        l16, r16 = left, right
        if pot_rows is not None:
            extra = pot_rows[safe]
            l16, r16 = left + extra, right + extra
        top = jnp.concatenate([w, zero], axis=1)
        mid = jnp.concatenate([zero, w], axis=1)
        low = jnp.concatenate([l16, r16], axis=1)
        rhs = jnp.concatenate([top, mid] + [low] * 8, axis=0)
        body = jnp.concatenate([lhs[jnp.minimum(q, NBLK - 1)] for q in ids], axis=0)
        tail = jnp.concatenate([aug[q] for q in ids], axis=0)
        both = jnp.concatenate([body, tail], axis=1)
        process[bank](p, jnp.dot(both, rhs, preferred_element_type=f32))

    count = table[0, LANES - 1]
    full = (count + BODY - 1 - 2 * REST) // BODY
    done = BODY * full

    @pl.loop(0, full)
    def _(turn):
        for k in range(BODY):
            work(BODY * turn + k, k % len(process))

    @pl.loop(0, jnp.maximum(count - done + REST - 1, 0) // REST)
    def _(turn):
        for k in range(REST):
            work(done + REST * turn + k, k % len(process))


def max_process(peak, total, piece):
    def process(p, v):
        old, sums = peak[p], total[p]
        for k in range(0, CHUNK * HALF, piece):
            u = v[k : k + piece].reshape(piece // 8, 8, 2 * BLK)
            top = jnp.max(u, axis=0)
            new = jnp.maximum(old, jnp.maximum(top[:, :BLK], top[:, BLK:]))
            new2 = jnp.concatenate([new, new], axis=1)
            e = jnp.sum(jnp.exp2((u - new2[None]) * C2), axis=0)
            sums = sums * jnp.exp2((old - new) * C2) + (e[:, :BLK] + e[:, BLK:])
            old = new
        peak[p] = old
        total[p] = sums

    return process


def sum_process(total):
    def process(p, v):
        u = v.reshape(CHUNK * HALF // 8, 8, 2 * BLK)
        e = jnp.sum(jnp.exp2(u * C2), axis=0)
        total[p] = total[p] + (e[:, :BLK] + e[:, BLK:])

    return process


def init_peaks(peak, total):
    peak[...] = jnp.full(peak.shape, LOW, f32)
    total[...] = jnp.zeros(total.shape, f32)


def finish_peaks(peak, total, *more):
    m, sums = peak[0:NBLK], total[0:NBLK]
    if more:
        old, other = m, more[0][0:NBLK]
        m = jnp.maximum(old, other)
        sums = sums * jnp.exp2((old - m) * C2) + more[1][0:NBLK] * jnp.exp2((other - m) * C2)
    top = jnp.max(m, axis=1)
    s = jnp.sum(sums * jnp.exp2((m - top[:, None, :]) * C2), axis=1)
    return top + jnp.log2(s) * (1.0 / C2)


def finish_total(total):
    return jnp.sum(total[0:NBLK], axis=1)


def x_weights(xt):
    return lambda p: xt[:, pl.ds(pl.multiple_of(p * BLK, BLK), BLK)]


def fetch(far, table, sem):
    copy = pltpu.make_async_copy(far, table, sem.at[0])
    copy.start()
    return copy


def row1_kernel(far, b, yfold, xt, peak, total, peak2, total2, aug, table, sem):
    listed = fetch(far, table, sem)
    fold_potential(b, aug)
    init_peaks(peak, total)
    init_peaks(peak2, total2)
    listed.wait()
    sweep(table, yfold, aug, x_weights(xt), None, [max_process(peak, total, 64), max_process(peak2, total2, 64)])


def col1_kernel(far, a, xfold, yt, peak, total, aug, table, sem):
    listed = fetch(far, table, sem)
    fold_potential(a, aug)
    init_peaks(peak, total)
    listed.wait()
    sweep(table, xfold, aug, lambda t: yt[t], None, [max_process(peak, total, 32)])


def row2_kernel(far, rows, b, yfold, xt, total, aug, table, sem):
    listed = fetch(far, table, sem)
    fold_potential(b, aug)
    total[...] = jnp.zeros(total.shape, f32)
    listed.wait()
    sweep(table, yfold, aug, x_weights(xt), rows, [sum_process(total)])


def col2_kernel(far, rows, a, xfold, yt, xsq, total, f_out, aug, table, sem, f, f_sem):
    listed = fetch(far, table, sem)
    f[...] = a[...] * (1.0 / 32) + xsq[...] * (1.0 / 64)
    leave = pltpu.make_async_copy(f, f_out, f_sem.at[0])
    leave.start()
    fold_potential(a, aug)
    total[...] = jnp.zeros(total.shape, f32)
    listed.wait()
    sweep(table, xfold, aug, lambda t: yt[t], rows, [sum_process(total)])
    leave.wait()


AUG = pltpu.VMEM((NBLK + 1, HALF, BLK), bf16)
ROWS = jax.ShapeDtypeStruct((NBLK, 16, BLK), bf16)
ACC = jax.ShapeDtypeStruct((NBLK + 1, 8, BLK), f32)
TABLE = jax.ShapeDtypeStruct((1, LANES), jnp.int32)


def work_call(kernel, outs, *args, out_specs=None, scratch=()):
    return pl.pallas_call(
        kernel,
        out_shape=outs,
        in_specs=[VMEM] * len(args),
        out_specs=out_specs or jax.tree.map(lambda _: VMEM, outs),
        scratch_shapes=[AUG, pltpu.SMEM(TABLE.shape, TABLE.dtype), pltpu.SemaphoreType.DMA((1,)), *scratch],
        compiler_params=params(),
    )(*args)


def duals(n=NBLK):
    return jax.ShapeDtypeStruct((n, BLK), f32)


def place():
    i = lax.axis_index("src")
    core, z, y = lax.rem(i, 2), lax.rem(i // 2, NZ), i // (2 * NZ)
    return y, z, core


def at(y, z, core):
    return {"src": (y * NZ + z) * 2 + core}


def hail(devices):
    barrier = pltpu.get_barrier_semaphore()
    for d in devices:
        pl.semaphore_signal(barrier, inc=1, device_id=d, device_id_type=MESH)


def meet(devices):
    pl.semaphore_wait(pltpu.get_barrier_semaphore(), len(devices))


def send(src, dst, sends, recvs, k, device):
    copy = pltpu.make_async_remote_copy(
        src_ref=src, dst_ref=dst, send_sem=sends.at[k], recv_sem=recvs.at[k],
        device_id=device, device_id_type=MESH,
    )
    copy.start()
    return copy


def slot_of(dz):
    return 2 * dz - 1 if 0 < dz <= 4 else 2 * (NZ - dz) if dz else 0


GROUPS = ((0, 1), (1, 2), (3, 2), (5, 2), (7, 1))


def gather_kernel(
    own, bt_far, xt_far, yt, yfold, b0, row_table, member_ref, xt,
    held, bt_ref, ls, zs, zr, ys, yr, cs, cr,
):
    y, z, core = place()
    pick = picker()
    z_devices = {k: at(y, lax.rem(z + k, NZ), core) for k in (4, 3, 5, 2, 6, 1, 7)}
    y_devices = {k: at(lax.rem(y + k, NY), z, core) for k in (2, 1, 3)}
    mate = at(y, z, 1 - core)
    everyone = list(z_devices.values()) + list(y_devices.values()) + [mate]
    mine = held.at[0, 0, 0]
    hail(everyone)
    here = [
        pltpu.make_async_copy(src, dst, ls.at[k])
        for k, (src, dst) in enumerate(((own, mine), (bt_far, bt_ref), (xt_far, xt)))
    ]
    for c in here:
        c.start()
    here[0].wait()
    meet(everyone)

    z_copies = {}
    for k, d in z_devices.items():
        z_copies[k] = send(mine, held.at[0, 0, slot_of(NZ - k)], zs, zr, k - 1, d)
    y_copies = {}

    def on_y(g):
        first, size = GROUPS[g]
        for k, d in y_devices.items():
            part = held.at[0, 0, pl.ds(first, size)]
            dst = held.at[0, NY - k, pl.ds(first, size)]
            y_copies[k, g] = send(part, dst, ys, yr, len(GROUPS) * (k - 1) + g, d)

    c_copies = []

    def on_mate(dy, dys, first, size):
        part = held.at[0, pl.ds(dy, dys), pl.ds(first, size)]
        dst = held.at[1, pl.ds(dy, dys), pl.ds(first, size)]
        c_copies.append(send(part, dst, cs, cr, len(c_copies), mate))

    def take(side, dy, s):
        dz = (s + 1) // 2 if s % 2 else NZ - s // 2
        who = core if side == 0 else 1 - core
        t = (lax.rem(y + dy, NY) * NZ + lax.rem(z + dz, NZ)) * 2 + who
        tile = held[side, dy, s]
        yt[t] = tile
        yfold[t] = fold(pick, tile)
        wide = tile.astype(f32)
        b0[pl.ds(t, 1), :] = -0.5 * jnp.sum(wide * wide, axis=0, keepdims=True)

    def take_column(side):
        for s in range(NZ):
            take(side, 0, s)

    def take_group(side, g):
        for s in range(GROUPS[g][0], GROUPS[g][0] + GROUPS[g][1]):
            for dy in range(1, NY):
                take(side, dy, s)

    on_y(0)
    def pass_on(g):
        for k in (1, 3, 2):
            y_copies[k, g].wait_recv()
        on_mate(1, NY - 1, *GROUPS[g])

    for g, ks in ((1, (1, 7)), (2, (2, 6)), (3, (3, 5)), (4, (4,))):
        for k in ks:
            z_copies[k].wait_recv()
        on_y(g)
        if g == 2:
            pass_on(0)
    on_mate(0, 1, 0, NZ)
    here[1].wait()
    t = iota((NBLK, NBLK), 0)
    bt = bt_ref[...]
    member = sum((bt[k : k + 1, :] == t).astype(f32) for k in range(SLOTS))
    eye = (iota((NBLK, NBLK), 1) == t).astype(bf16)
    member_ref[...] = member
    row_table[...] = chunk_table(turn_over(eye, member.astype(bf16)))
    take_column(0)
    take_group(0, 0)
    pass_on(1)
    take_group(0, 1)
    c_copies[0].wait_recv()
    take_group(1, 0)
    pass_on(2)
    take_group(0, 2)
    c_copies[1].wait_recv()
    take_column(1)
    pass_on(3)
    take_group(0, 3)
    c_copies[2].wait_recv()
    take_group(1, 1)
    pass_on(4)
    take_group(0, 4)
    for g in range(2, 5):
        c_copies[1 + g].wait_recv()
        take_group(1, g)
    here[2].wait()
    for c in list(z_copies.values()) + list(y_copies.values()) + c_copies:
        c.wait_send()


def gather(own, bt, xt):
    dma = pltpu.SemaphoreType.DMA
    blocks = jax.ShapeDtypeStruct((NBLK, DIM, BLK), bf16)
    return pl.pallas_call(
        gather_kernel,
        out_shape=(blocks, blocks, duals(), TABLE, jax.ShapeDtypeStruct((NBLK, NBLK), f32), jax.ShapeDtypeStruct(xt.shape, bf16)),
        in_specs=[pl.BlockSpec(memory_space=pl.ANY)] * 3,
        out_specs=(VMEM,) * 6,
        scratch_shapes=[pltpu.VMEM((2, NY, NZ, DIM, BLK), bf16), pltpu.VMEM(bt.shape, jnp.int32)]
        + [dma((3,)), dma((7,)), dma((7,)), dma((15,)), dma((15,)), dma((6,)), dma((6,))],
        compiler_params=params(0, 50),
    )(own, bt, xt)


def spread(pairs, device_of, sends, recvs):
    for k, (src, dst) in enumerate(pairs):
        pltpu.make_async_remote_copy(
            src_ref=src, dst_ref=dst, send_sem=sends.at[0], recv_sem=recvs.at[0],
            device_id=device_of[k], device_id_type=MESH,
        ).start()


def collect(many, device, sends, recvs):
    pltpu.make_async_remote_copy(
        src_ref=many, dst_ref=many, send_sem=sends.at[0], recv_sem=recvs.at[0],
        device_id=device, device_id_type=MESH,
    ).wait()


def tgt_exchange(finish, meanwhile, mine, got, sends, recvs):
    me = lax.axis_index("tgt")
    devices = [{"tgt": lax.rem(me + k, NX)} for k in (2, 1, 3)]
    hail(devices)
    mine[...] = finish().astype(mine.dtype)
    meet(devices)
    spread([(mine, got.at[me])] * 3, devices, sends, recvs)
    got[me] = mine[...]
    meanwhile()
    collect(got.at[pl.ds(0, 3)], devices[0], sends, recvs)


def tgt1_kernel(peak, total, peak2, total2, xt, member, a_ref, xfold, xsq, col_table, mine, got, sends, recvs):
    pick = picker()

    def meanwhile():
        col_table[...] = chunk_table(member[...])

        @pl.loop(0, NBLK, step=8)
        def _(p):
            for i in range(8):
                tile = xt[:, pl.ds(pl.multiple_of((p + i) * BLK, BLK), BLK)]
                xfold[p + i] = fold(pick, tile)
                wide = tile.astype(f32)
                xsq[pl.ds(p + i, 1), :] = jnp.sum(wide * wide, axis=0, keepdims=True)

    tgt_exchange(lambda: finish_peaks(peak, total, peak2, total2), meanwhile, mine, got, sends, recvs)
    a_ref[...] = -lse([got[k] for k in range(NX)]) - LOG_NS


def tgt2_kernel(total, old, b_ref, a_ref, rows, mine, got, sends, recvs):
    tgt_exchange(
        lambda: finish_total(total), lambda: spread_rows(b_ref, rows), mine, got, sends, recvs
    )
    g0, g1, g2, g3 = (got[k].astype(f32) for k in range(NX))
    s = (g0 + g1) + (g2 + g3)
    a_ref[...] = old[...] - jnp.log2(s * NS) * (1.0 / C2)


def tgt_call(kernel, collective_id, kind, outs, *args):
    dma = pltpu.SemaphoreType.DMA
    mine = pltpu.VMEM((NBLK, BLK), kind)
    return pl.pallas_call(
        kernel,
        out_shape=outs,
        in_specs=[VMEM] * len(args),
        out_specs=jax.tree.map(lambda _: VMEM, outs),
        scratch_shapes=[mine, pltpu.VMEM((NX, NBLK, BLK), kind), dma((1,)), dma((1,))],
        compiler_params=params(collective_id),
    )(*args)


def lse(parts):
    top = functools.reduce(jnp.maximum, parts)
    s = sum(jnp.exp2((v - top) * C2) for v in parts)
    return top + jnp.log2(s) * (1.0 / C2)


def mates():
    y, z, core = place()
    m = y * 2 + core

    def side(k):
        other = lax.rem(m + k, 8)
        return other, at(other // 2, z, lax.rem(other, 2))

    def up(k):
        other = lax.rem(z + k, NZ)
        return other, at(y, other, core)

    far_first = (4, 3, 5, 2, 6, 1, 7)
    return m, z, [side(k) for k in far_first], [up(k) for k in far_first]


def rows_of(k):
    return pl.ds((k // 2) * 2 * NZ + k % 2, NZ, stride=2)


def scatter_sides(finish, combine, m, sides, ups, mine, order, r1, sends, recvs):
    devices = [d for _, d in ups + sides]
    hail(devices)
    mine[...] = finish()
    for k in range(8):
        order[k] = mine[rows_of(k), :]
    meet(devices)
    spread([(order.at[o], r1.at[m]) for o, _ in sides], [d for _, d in sides], sends, recvs)
    r1[m] = order[m]
    collect(r1.at[pl.ds(0, 7)], sides[0][1], sends, recvs)
    return combine([r1[k] for k in range(8)])


def src1_kernel(peak, total, a_ref, b_ref, own_ref, a_rows, mine, order, r1, tile, r2, done, r4, s1, q1, s2, q2, s3, q3):
    m, z, sides, ups = mates()
    tile[...] = scatter_sides(
        lambda: finish_peaks(peak, total), lse, m, sides, ups, mine, order, r1, s1, q1
    )
    spread([(tile, r2.at[z])] * 7, [d for _, d in ups], s2, q2)
    r2[z] = tile[...]
    spread_rows(a_ref, a_rows)
    collect(r2.at[pl.ds(0, 7)], ups[0][1], s2, q2)
    done[...] = -lse([r2[k] for k in range(8)]) - LOG_NT
    spread([(done, r4.at[m])] * 7, [d for _, d in sides], s3, q3)
    r4[m] = done[...]
    own_ref[...] = jnp.broadcast_to(done[pl.ds(z, 1), :], (8, BLK))
    collect(r4.at[pl.ds(0, 7)], sides[0][1], s3, q3)
    for k in range(8):
        b_ref[rows_of(k), :] = r4[k]


def src2_kernel(total, old, yt_ref, g_ref, mine, order, r1, rows, r2, s1, q1, s2, q2):
    m, z, sides, ups = mates()
    first = scatter_sides(
        lambda: finish_total(total), sum, m, sides, ups, mine, order, r1, s1, q1
    )
    for k in range(8):
        rows[k] = jnp.broadcast_to(first[k : k + 1], (8, BLK))
    spread([(rows.at[o], r2.at[z]) for o, _ in ups], [d for _, d in ups], s2, q2)
    r2[z] = rows[z]
    y = yt_ref[...].astype(f32)
    sq = jnp.sum(y * y, axis=0, keepdims=True)
    collect(r2.at[pl.ds(0, 7)], ups[0][1], s2, q2)
    s = sum([r2[k] for k in range(8)])
    b = old[...] - jnp.log2(s * NT) * (1.0 / C2)
    g_ref[...] = b * (1.0 / 32) + sq * (1.0 / 64)


def src_call(kernel, collective_id, outs, scratch, phases, *args):
    mine = pltpu.VMEM((NBLK, BLK), f32)
    return pl.pallas_call(
        kernel,
        out_shape=outs,
        in_specs=[VMEM] * len(args),
        out_specs=jax.tree.map(lambda _: VMEM, outs),
        scratch_shapes=[mine] + scratch + [pltpu.SemaphoreType.DMA((1,))] * (2 * phases),
        compiler_params=params(collective_id),
    )(*args)


def local(source_features, target_features, block_targets):
    own_yt = target_features[0].T
    block, tile = pltpu.VMEM((8, 8, BLK), f32), pltpu.VMEM((8, BLK), f32)

    blocks = jax.ShapeDtypeStruct((NBLK, DIM, BLK), bf16)
    yt, yfold, b0, row_table, member, xt = gather(
        own_yt, block_targets[:, 0, :].T, source_features.T
    )
    sums = work_call(row1_kernel, (ACC,) * 4, row_table, b0, yfold, xt)
    a, xfold, xsq, col_table = tgt_call(
        tgt1_kernel, 1, f32, (duals(), blocks, duals(), TABLE), *sums, xt, member
    )
    peak, total = work_call(col1_kernel, (ACC, ACC), col_table, a, xfold, yt)
    b, own, rows = src_call(
        src1_kernel, 2, (duals(), duals(8), ROWS), [block, block, tile, block, tile, block], 3,
        peak, total, a,
    )
    total = work_call(row2_kernel, ACC, row_table, rows, b, yfold, xt)
    a, rows = tgt_call(tgt2_kernel, 3, bf16, (duals(), ROWS), total, a, b)
    total, f = work_call(
        col2_kernel, (ACC, duals()), col_table, rows, a, xfold, yt, xsq,
        out_specs=(VMEM, pl.BlockSpec(memory_space=pl.ANY)),
        scratch=(pltpu.VMEM((NBLK, BLK), f32), pltpu.SemaphoreType.DMA((1,))),
    )
    g = src_call(src2_kernel, 4, duals(8), [block] * 4, 2, total, own, own_yt)
    return f.reshape(-1), g[0:1]


def solution(mesh):
    in_specs = (P("src", None), P("tgt", "src", None), P("src", "tgt", None))
    out_specs = (P("src"), P("tgt", "src"))
    return jax.shard_map(local, mesh=mesh, in_specs=in_specs, out_specs=out_specs, check_vma=False)
```
